32 devices in a mesh: band: 16 (over z, x, core), var: 2 (over y).
Axes of the slice: x: 2, y: 2, z: 4, core: 2. Of those that a mesh axis runs over, the one named last changes fastest.
Arguments:
- patches: bfloat16 [16, 16, 64, 64], P('var', 'band'), may hold values from -6 to 6
- w_embed: bfloat16 [16, 64, 2048], P('var'), may hold values from -0.75 to 0.75
- var_bias: float32 [16, 2048], P('var'), may hold values from -3 to 3
- agg_gain: float32 [2048], replicated, may hold values from 0.1 to 1.9
- wq: bfloat16 [2048, 2048], P(None, 'var'), may hold values from -4 to 4
- wk: bfloat16 [2048, 2048], P(None, 'var'), may hold values from -4 to 4
- wv: bfloat16 [2048, 2048], P(None, 'var'), may hold values from -0.125 to 0.125
- wo: bfloat16 [2048, 2048], P('var'), may hold values from -0.125 to 0.125
- w_up: bfloat16 [2048, 1024], replicated, may hold values from -0.125 to 0.125
- conv1: bfloat16 [9, 64, 64], replicated, may hold values from -0.25 to 0.25
- bias1: float32 [64], replicated, may hold values from -3 to 3
- conv2: bfloat16 [9, 64, 64], replicated, may hold values from -0.25 to 0.25
- cotangent: bfloat16 [64, 64, 256], P('band', None, 'var'), may hold values from -6 to 6
Outputs:
- field_out: bfloat16 [64, 64, 256], P('band', None, 'var')
- grad_fine: bfloat16 [64, 64, 256], P('band', None, 'var')
- grad_conv1: float32 [9, 64, 64], replicated
- grad_conv2: float32 [9, 64, 64], replicated
- grad_bias: float32 [64], replicated
The draws below stay inside these ranges and needn't reach their ends.
All inputs are finite; a program needn't handle non-finite values.
Results may differ from the reference program's by a relative error of at most 0.03.
Values may be sent and summed in bfloat16 or wider, within the bound.
A program may use at most 128 MiB of HBM per device.

```python
import math
import jax
import jax.numpy as jnp
from jax import lax

D = 2048
HEADS = 16
HD = 128
VARS = 16
P_SIZE = 64
C = 64
R = 4
LAT = 16
LON = 64
TOKENS = 1024
FY = 64
FX = 256


def projection_pair(key):
    folded = jax.random.fold_in(key, 4242)
    first_key, second_key, third_key, fourth_key = jax.random.split(folded, 4)
    columns = HEADS * HD
    query_part = jax.random.normal(first_key, (D, columns), jnp.float32) / jnp.sqrt(jnp.float32(D))
    key_part = jax.random.normal(second_key, (D, columns), jnp.float32) / jnp.sqrt(jnp.float32(D))
    strength = jnp.exp(jax.random.uniform(fourth_key, (HEADS,), jnp.float32, math.log(1.5), math.log(4.0)))
    head_sign = (jax.random.randint(third_key, (HEADS,), 0, 2) * 2 - 1).astype(jnp.float32)
    key_part = jnp.repeat(head_sign * strength, HD)[None, :] * query_part + key_part
    return (jnp.clip(query_part, -4.0, 4.0), jnp.clip(key_part, -4.0, 4.0))


def draw_wq(key, part):
    return projection_pair(key)[0].astype(jnp.bfloat16)


def draw_wk(key, part):
    return projection_pair(key)[1].astype(jnp.bfloat16)


def draw_patches(key, part):
    folded = jax.random.fold_in(key, 777)
    order_key, shared_key, own_key = jax.random.split(folded, 3)
    order = jax.random.permutation(order_key, TOKENS)
    ranks = jnp.zeros((TOKENS,), jnp.int32).at[order].set(jnp.arange(TOKENS, dtype=jnp.int32))
    groups = ranks // 4
    token_sign = jnp.where(ranks % 4 < 2, 1.0, -1.0).astype(jnp.float32)
    shared = jax.random.normal(shared_key, (VARS, TOKENS // 4, P_SIZE), jnp.float32)
    own = jax.random.normal(own_key, (VARS, TOKENS, P_SIZE), jnp.float32)
    spread = jnp.take(shared, groups, axis=1)
    values = math.sqrt(0.9) * token_sign[None, :, None] * spread + math.sqrt(0.1) * own
    return jnp.clip(values, -6.0, 6.0).reshape(VARS, LAT, LON, P_SIZE).astype(jnp.bfloat16)


def with_spikes(array, stream_key, source, target, parts, factor):
    owner, partner = [(jnp.arange(array.shape[axis_at]) // (array.shape[axis_at] // parts)).reshape([-1 if axis == axis_at else 1 for axis in range(array.ndim)]) for axis_at in (source, target)]
    chosen = jax.random.permutation(stream_key, parts)[partner]
    strong = (owner == chosen) | (owner == (partner + parts // 2) % parts)
    return jnp.where(strong, factor * array, array)


def levels(key, extent, cuts, least, largest):
    def one(position, parts):
        draws = jax.random.uniform(jax.random.fold_in(jax.random.fold_in(key, 6), position), (parts,), jnp.float32, least / len(cuts), largest / len(cuts))
        return jnp.repeat(jnp.exp(draws), extent[position] // parts).reshape((-1,) + (1,) * (len(extent) - position - 1))

    loudness = one(*cuts[0])
    for cut in cuts[1:]:
        loudness = loudness * one(*cut)
    return loudness


def bell_draw(key, extent, deviation, most, cuts=(), kind=jnp.bfloat16):
    entries = jax.random.normal(key, extent, jnp.float32) * deviation
    if len(cuts) > 0:
        entries = levels(key, extent, cuts, -0.22, 0.18) * entries
    return jnp.clip(entries, min=-most, max=most).astype(kind)


def noise_with(key, extent, scale, limit, cuts, heavy, kind=jnp.bfloat16):
    drawn = scale * jax.random.normal(key, extent, jnp.float32)
    if cuts:
        drawn = drawn * levels(key, extent, cuts, -0.22, 0.18)
    return jnp.clip(with_spikes(drawn, jax.random.fold_in(key, 3), *heavy), -limit, limit).astype(kind)


def setup_inputs(seed: int = 0) -> dict:
    key_list = jax.random.split(jax.random.key(seed), 14)
    patches = draw_patches(jax.random.fold_in(key_list[13], 71), 0)
    w_embed = bell_draw(key_list[1], (VARS, P_SIZE, D), P_SIZE ** -0.5, 0.75, ((0, 2),))
    var_bias = bell_draw(key_list[2], (VARS, D), 0.5, 3.0, ((0, 2),), jnp.float32)
    agg_gain = jnp.clip(1.0 + 0.18 * jax.random.normal(key_list[3], (D,), jnp.float32), 0.1, 1.9)
    wq = draw_wq(jax.random.fold_in(key_list[13], 71), 0)
    wk = draw_wk(jax.random.fold_in(key_list[13], 71), 0)
    wv = bell_draw(key_list[6], (D, HEADS * HD), D ** -0.5, 0.125, ((1, 2),))
    wo = bell_draw(key_list[7], (HEADS * HD, D), (HEADS * HD) ** -0.5, 0.125, ((0, 2),))
    w_up = bell_draw(key_list[8], (D, R * R * C), D ** -0.5, 0.125)
    conv1 = bell_draw(key_list[9], (9, C, C), (9 * C) ** -0.5, 0.25)
    bias1 = bell_draw(key_list[10], (C,), 0.5, 3.0, (), jnp.float32)
    conv2 = bell_draw(key_list[11], (9, C, C), (9 * C) ** -0.5, 0.25)
    cotangent = noise_with(key_list[12], (FY, C, FX), 1.0, 6.0, ((0, 16), (2, 2)), (0, 1, 16, 2.0))
    return dict(patches=patches, w_embed=w_embed, var_bias=var_bias, agg_gain=agg_gain, wq=wq, wk=wk, wv=wv, wo=wo, w_up=w_up, conv1=conv1, bias1=bias1, conv2=conv2, cotangent=cotangent)


def tap_stack(padded, height, width):
    pieces = [padded[row_tap:row_tap + height, :, col_tap:col_tap + width] for row_tap in range(3) for col_tap in range(3)]
    return jnp.concatenate(pieces, axis=1)

def conv_apply(field, weight):
    padded = jnp.pad(field, ((1, 1), (0, 0), (1, 1)))
    stacked = tap_stack(padded, field.shape[0], field.shape[2]).astype(jnp.float32)
    return jnp.einsum('ykx,ko->yox', stacked, weight.reshape(-1, weight.shape[2]).astype(jnp.float32))

def flipped(weight):
    return jnp.transpose(weight[::-1], (0, 2, 1))

def weight_grad(field, grads):
    padded = jnp.pad(field, ((1, 1), (0, 0), (1, 1)))
    stacked = tap_stack(padded, field.shape[0], field.shape[2]).astype(jnp.float32)
    summed = jnp.einsum('ykx,yox->ko', stacked, grads.astype(jnp.float32))
    return summed.reshape(9, field.shape[1], grads.shape[1])

def head_attention(inputs):
    query_head, key_head, value_head = inputs
    block = math.gcd(TOKENS, 1024)
    blocks = query_head.reshape(TOKENS // block, block, HD)
    key_float = key_head.astype(jnp.float32)

    def one_block(query_block):
        scores = jnp.dot(query_block.astype(jnp.float32), key_float.T, preferred_element_type=jnp.float32) / math.sqrt(HD)
        weights = jnp.exp(scores - lax.optimization_barrier(jnp.max(scores, axis=1, keepdims=True)))
        numer = jnp.dot(weights.astype(jnp.bfloat16), value_head, preferred_element_type=jnp.float32)
        return (numer / lax.optimization_barrier(jnp.sum(weights, axis=1, keepdims=True))).astype(jnp.bfloat16)
    return lax.map(one_block, blocks).reshape(TOKENS, HD)

def split_heads(matrix):
    return jnp.transpose(matrix.reshape(TOKENS, HEADS, HD), (1, 0, 2))

def reference(patches, w_embed, var_bias, agg_gain, wq, wk, wv, wo, w_up, conv1, bias1, conv2, cotangent):
    flattened = jnp.transpose(patches, (1, 2, 0, 3)).reshape(LAT * LON, VARS * P_SIZE)
    mixed = jnp.dot(flattened, w_embed.reshape(VARS * P_SIZE, D), preferred_element_type=jnp.float32) + lax.optimization_barrier(jnp.sum(var_bias, axis=0))
    normed = (mixed * lax.rsqrt(lax.optimization_barrier(jnp.mean(mixed * mixed, axis=1, keepdims=True)) + 1e-05) * agg_gain).astype(jnp.bfloat16)
    queries = jnp.dot(normed, wq, preferred_element_type=jnp.float32).astype(jnp.bfloat16)
    keys_all = jnp.dot(normed, wk, preferred_element_type=jnp.float32).astype(jnp.bfloat16)
    values_all = jnp.dot(normed, wv, preferred_element_type=jnp.float32).astype(jnp.bfloat16)
    context = lax.map(head_attention, (split_heads(queries), split_heads(keys_all), split_heads(values_all)))
    context = jnp.transpose(context, (1, 0, 2)).reshape(TOKENS, HEADS * HD)
    hidden = (normed.astype(jnp.float32) + jnp.dot(context, wo, preferred_element_type=jnp.float32)).astype(jnp.bfloat16)
    upsampled = jnp.dot(hidden, w_up, preferred_element_type=jnp.float32).astype(jnp.bfloat16)
    upsampled = jnp.transpose(upsampled.reshape(LAT, LON, R, R, C), (0, 2, 4, 1, 3)).reshape(FY, C, FX)
    pre = conv_apply(upsampled, conv1) + bias1[None, :, None]
    active = jax.nn.gelu(pre).astype(jnp.bfloat16)
    field_out = (conv_apply(active, conv2) + upsampled.astype(jnp.float32)).astype(jnp.bfloat16)
    d_active = conv_apply(cotangent, flipped(conv2))
    d_pre = jax.vjp(jax.nn.gelu, pre)[1](d_active)[0].astype(jnp.bfloat16)
    grad_fine = (cotangent.astype(jnp.float32) + conv_apply(d_pre, flipped(conv1))).astype(jnp.bfloat16)
    factor = 1.0 / math.sqrt(FY * FX)
    grad_conv1 = weight_grad(upsampled, d_pre) * factor
    grad_conv2 = weight_grad(active, cotangent) * factor
    grad_bias = lax.optimization_barrier(jnp.sum(d_pre.astype(jnp.float32), axis=(0, 2))) * factor
    return (field_out, grad_fine, grad_conv1, grad_conv2, grad_bias)
```

```python
import functools
import math

import jax
import jax.numpy as jnp
from jax import lax
from jax.experimental import pallas as pl
from jax.experimental.pallas import tpu as pltpu
from jax.sharding import PartitionSpec as P

MESH = pl.DeviceIdType.MESH

D = 2048
HD = 128
C = 64
R = 4


def with_halo(cells, sides, width):
    for axis, dim in sides:
        count = lax.axis_size(axis)
        ends = count - 1
        head = lax.slice_in_dim(cells, 0, width, axis=dim)
        tail = lax.slice_in_dim(cells, cells.shape[dim] - width, cells.shape[dim], axis=dim)
        cells = jnp.concatenate(
            [
                lax.ppermute(tail, axis, [(i, (i + 1) % count) for i in range(ends)]),
                cells,
                lax.ppermute(head, axis, [((i + 1) % count, i) for i in range(ends)]),
            ],
            axis=dim,
        )
    return cells


def tap_stack(padded, height, width):
    pieces = [
        padded[row_tap : row_tap + height, :, col_tap : col_tap + width]
        for row_tap in range(3)
        for col_tap in range(3)
    ]
    return jnp.concatenate(pieces, axis=1)


def conv_padded(padded, weight, height, width):
    stacked = tap_stack(padded, height, width)
    return jnp.einsum(
        "ykx,ko->yox",
        stacked,
        weight.reshape(-1, weight.shape[2]),
        preferred_element_type=jnp.float32,
    )


def flipped(weight):
    return jnp.transpose(weight[::-1], (0, 2, 1))


def weight_grad(padded, grads):
    stacked = tap_stack(padded, grads.shape[0], grads.shape[2])
    summed = jnp.einsum("ykx,yox->ko", stacked, grads, preferred_element_type=jnp.float32)
    return summed.reshape(9, padded.shape[1], grads.shape[1])


def normalize(mixed, agg_gain):
    return (
        mixed * lax.rsqrt(jnp.mean(mixed * mixed, axis=-1, keepdims=True) + 1e-05) * agg_gain
    ).astype(jnp.bfloat16)


def gradient_rim(field):
    return with_halo(field, (("band", 0), ("var", 2)), 1)


def sum_kernel(count, var_count, x_ref, o_ref, landed, send1, recv1, send2, recv2):
    me = lax.axis_index("band") * var_count + lax.axis_index("var")

    def place(device):
        return (lax.div(device, var_count), lax.rem(device, var_count))

    def scatter(step):
        peer = lax.rem(me + step, count)
        return pltpu.make_async_remote_copy(
            src_ref=x_ref.at[peer],
            dst_ref=landed.at[step],
            send_sem=send1.at[step],
            recv_sem=recv1.at[step],
            device_id=place(peer),
            device_id_type=MESH,
        )

    def spread(step, owner):
        return pltpu.make_async_remote_copy(
            src_ref=o_ref.at[owner],
            dst_ref=o_ref.at[owner],
            send_sem=send2.at[step],
            recv_sem=recv2.at[step],
            device_id=place(lax.rem(me + step, count)),
            device_id_type=MESH,
        )

    barrier = pltpu.get_barrier_semaphore()

    @pl.loop(1, count)
    def _(step):
        pl.semaphore_signal(
            barrier, inc=1, device_id=place(lax.rem(me + step, count)), device_id_type=MESH
        )

    pl.semaphore_wait(barrier, count - 1)

    @pl.loop(1, count)
    def _(step):
        scatter(step).start()

    def add(step, total):
        scatter(step).wait_recv()
        return total + landed[step]

    o_ref[me] = lax.fori_loop(1, count, add, x_ref[me])

    @pl.loop(1, count)
    def _(step):
        spread(step, me).start()

    @pl.loop(1, count)
    def _(step):
        spread(step, lax.rem(me - step + count, count)).wait_recv()

    @pl.loop(1, count)
    def _(step):
        scatter(step).wait_send()
        spread(step, me).wait_send()


def sum_everywhere(terms, band_count, var_count):
    count = band_count * var_count
    rows = -(-terms.shape[0] // (8 * count)) * 8
    padded = jnp.pad(terms, ((0, rows * count - terms.shape[0]), (0, 0)))
    slots = (count, rows, terms.shape[1])
    summed = pl.pallas_call(
        functools.partial(sum_kernel, count, var_count),
        out_shape=jax.ShapeDtypeStruct(slots, jnp.float32),
        in_specs=[pl.BlockSpec(memory_space=pltpu.VMEM)],
        out_specs=pl.BlockSpec(memory_space=pltpu.VMEM),
        scratch_shapes=[pltpu.VMEM(slots, jnp.float32)]
        + [pltpu.SemaphoreType.DMA((count,)) for _ in range(4)],
        compiler_params=pltpu.CompilerParams(
            collective_id=0, has_side_effects=True, vmem_limit_bytes=32 << 20
        ),
    )(padded.reshape(slots))
    return summed.reshape(rows * count, terms.shape[1])


def on_device(
    patches, w_embed, var_bias, agg_gain, wq, wk, wv, wo, w_up, conv1, bias1, conv2, cotangent
):
    var_count = lax.axis_size("var")
    band_count = lax.axis_size("band")
    var_local, lat_dev, lon_all, patch_len = patches.shape
    lon_dev = lon_all // var_count
    flattened = jnp.transpose(patches, (1, 2, 0, 3)).reshape(
        lat_dev * lon_all, var_local * patch_len
    )
    partial_mix = jnp.dot(
        flattened, w_embed.reshape(var_local * patch_len, D), preferred_element_type=jnp.float32
    )
    partial_mix = (partial_mix + jnp.sum(var_bias, axis=0)).reshape(lat_dev, lon_all, D)
    own_mix = partial_mix.astype(jnp.bfloat16)
    if var_count == 2:
        other_mix = lax.ppermute(own_mix, "var", [(0, 1), (1, 0)])
        mixed = own_mix.astype(jnp.float32) + other_mix.astype(jnp.float32)
    else:
        mixed = lax.psum(own_mix, "var").astype(jnp.float32)
    normed_band = normalize(mixed, agg_gain)
    normed_slab = lax.dynamic_slice_in_dim(normed_band, lax.axis_index("var") * lon_dev, lon_dev, 1)
    token_rows = jnp.transpose(
        normed_band.reshape(lat_dev, var_count, lon_dev, D), (1, 0, 2, 3)
    ).reshape(-1, D)
    heads_local = wq.shape[1] // HD
    query_rows = token_rows.shape[0]
    queries = jnp.dot(token_rows, wq, preferred_element_type=jnp.float32).astype(jnp.bfloat16)
    keys_local = jnp.dot(token_rows, wk, preferred_element_type=jnp.float32).astype(jnp.bfloat16)
    values_local = jnp.dot(token_rows, wv, preferred_element_type=jnp.float32).astype(jnp.bfloat16)
    query_heads = queries.reshape(query_rows, heads_local, HD)
    running_max = jnp.full((heads_local, query_rows), -1e30, jnp.float32)
    key_heads = lax.all_gather(keys_local, "band", axis=0, tiled=True).reshape(-1, heads_local, HD)
    value_heads = lax.all_gather(values_local, "band", axis=0, tiled=True).reshape(
        -1, heads_local, HD
    )
    scores = jnp.einsum(
        "qhd,khd->hqk", query_heads, key_heads, preferred_element_type=jnp.float32
    ) / math.sqrt(HD)
    new_max = jnp.maximum(running_max, jnp.max(scores, axis=2))
    weights = jnp.exp(scores - new_max[:, :, None])
    new_sum = jnp.sum(weights, axis=2)
    update = jnp.einsum(
        "hqk,khd->hqd",
        weights.astype(jnp.bfloat16),
        value_heads,
        preferred_element_type=jnp.float32,
    )
    context = (update / new_sum[:, :, None]).astype(jnp.bfloat16)
    context = jnp.transpose(context, (1, 0, 2)).reshape(query_rows, heads_local * HD)
    slab_rows = lat_dev * lon_dev
    attended = lax.psum_scatter(
        jnp.dot(context, wo, preferred_element_type=jnp.float32).astype(jnp.bfloat16),
        "var",
        scatter_dimension=0,
        tiled=True,
    ).astype(jnp.float32)
    hidden = (normed_slab.reshape(slab_rows, D).astype(jnp.float32) + attended).astype(jnp.bfloat16)
    upsampled = jnp.dot(hidden, w_up, preferred_element_type=jnp.float32).astype(jnp.bfloat16)
    height = lat_dev * R
    width = lon_dev * R
    upsampled = jnp.transpose(
        upsampled.reshape(lat_dev, lon_dev, R, R, C), (0, 2, 4, 1, 3)
    ).reshape(height, C, width)
    bias_cols = bias1[None, :, None]
    widened = with_halo(upsampled, (("band", 0), ("var", 2)), 2)
    pre_wide = conv_padded(widened, conv1, height + 2, width + 2) + bias_cols
    row_ids = lax.axis_index("band") * height + jnp.arange(height + 2) - 1
    col_ids = lax.axis_index("var") * width + jnp.arange(width + 2) - 1
    rows_inside = (row_ids >= 0) & (row_ids < height * band_count)
    cols_inside = (col_ids >= 0) & (col_ids < width * var_count)
    inside = rows_inside[:, None, None] & cols_inside[None, None, :]
    active_pad = jnp.where(inside, jax.nn.gelu(pre_wide), 0.0).astype(jnp.bfloat16)
    fine_pad = widened[1:-1, :, 1:-1]
    pre = pre_wide[1:-1, :, 1:-1]
    field_out = (
        conv_padded(active_pad, conv2, height, width) + upsampled.astype(jnp.float32)
    ).astype(jnp.bfloat16)
    cotangent_pad = gradient_rim(cotangent)
    d_active = conv_padded(cotangent_pad, flipped(conv2), height, width)
    d_pre = jax.vjp(jax.nn.gelu, pre)[1](d_active)[0].astype(jnp.bfloat16)
    d_pre_pad = gradient_rim(d_pre)
    grad_fine = (
        cotangent.astype(jnp.float32) + conv_padded(d_pre_pad, flipped(conv1), height, width)
    ).astype(jnp.bfloat16)
    factor = 1.0 / math.sqrt(height * band_count * width * var_count)
    first_terms = weight_grad(fine_pad, d_pre).reshape(9 * C, C) * factor
    second_terms = weight_grad(active_pad, cotangent).reshape(9 * C, C) * factor
    bias_terms = jnp.sum(d_pre.astype(jnp.float32), axis=(0, 2)) * factor
    terms = jnp.concatenate([first_terms, second_terms], axis=1)
    bias_row = jnp.pad(bias_terms, (0, C))[None]
    summed = sum_everywhere(jnp.concatenate([terms, bias_row], axis=0), band_count, var_count)
    grad_conv1 = summed[: 9 * C, :C].reshape(9, C, C)
    grad_conv2 = summed[: 9 * C, C:].reshape(9, C, C)
    grad_bias = summed[9 * C, :C]
    return (field_out, grad_fine, grad_conv1, grad_conv2, grad_bias)


def solution(mesh):
    in_specs = (
        P("var", "band", None, None),
        P("var", None, None),
        P("var", None),
        P(),
        P(None, "var"),
        P(None, "var"),
        P(None, "var"),
        P("var", None),
        P(),
        P(),
        P(),
        P(),
        P("band", None, "var"),
    )
    out_specs = (P("band", None, "var"), P("band", None, "var"), P(), P(), P())
    return jax.shard_map(
        on_device, mesh=mesh, in_specs=in_specs, out_specs=out_specs, check_vma=False
    )
```

```python
import functools
import math

import jax
import jax.numpy as jnp
from jax import lax
from jax.experimental import pallas as pl
from jax.experimental.pallas import tpu as pltpu
from jax.sharding import PartitionSpec as P

MESH = pl.DeviceIdType.MESH

D = 2048
HD = 128
C = 64
R = 4


def with_halo(cells, sides, width):
    for axis, dim in sides:
        count = lax.axis_size(axis)
        ends = count - 1
        head = lax.slice_in_dim(cells, 0, width, axis=dim)
        tail = lax.slice_in_dim(cells, cells.shape[dim] - width, cells.shape[dim], axis=dim)
        cells = jnp.concatenate(
            [
                lax.ppermute(tail, axis, [(i, (i + 1) % count) for i in range(ends)]),
                cells,
                lax.ppermute(head, axis, [((i + 1) % count, i) for i in range(ends)]),
            ],
            axis=dim,
        )
    return cells


def tap_stack(padded, height, width):
    pieces = [
        padded[row_tap : row_tap + height, :, col_tap : col_tap + width]
        for row_tap in range(3)
        for col_tap in range(3)
    ]
    return jnp.concatenate(pieces, axis=1)


def conv_padded(padded, weight, height, width):
    stacked = tap_stack(padded, height, width)
    return jnp.einsum(
        "ykx,ko->yox",
        stacked,
        weight.reshape(-1, weight.shape[2]),
        preferred_element_type=jnp.float32,
    )


def flipped(weight):
    return jnp.transpose(weight[::-1], (0, 2, 1))


def weight_grad(padded, grads):
    stacked = tap_stack(padded, grads.shape[0], grads.shape[2])
    summed = jnp.einsum("ykx,yox->ko", stacked, grads, preferred_element_type=jnp.float32)
    return summed.reshape(9, padded.shape[1], grads.shape[1])


def gradient_rim(field):
    return with_halo(field, (("band", 0), ("var", 2)), 1)


def sum_kernel(count, var_count, x_ref, o_ref, landed, send1, recv1, send2, recv2):
    me = lax.axis_index("band") * var_count + lax.axis_index("var")

    def place(device):
        return (lax.div(device, var_count), lax.rem(device, var_count))

    def scatter(step):
        peer = lax.rem(me + step, count)
        return pltpu.make_async_remote_copy(
            src_ref=x_ref.at[peer],
            dst_ref=landed.at[step],
            send_sem=send1.at[step],
            recv_sem=recv1.at[step],
            device_id=place(peer),
            device_id_type=MESH,
        )

    def spread(step, owner):
        return pltpu.make_async_remote_copy(
            src_ref=o_ref.at[owner],
            dst_ref=o_ref.at[owner],
            send_sem=send2.at[step],
            recv_sem=recv2.at[step],
            device_id=place(lax.rem(me + step, count)),
            device_id_type=MESH,
        )

    barrier = pltpu.get_barrier_semaphore()

    @pl.loop(1, count)
    def _(step):
        pl.semaphore_signal(
            barrier, inc=1, device_id=place(lax.rem(me + step, count)), device_id_type=MESH
        )

    pl.semaphore_wait(barrier, count - 1)

    @pl.loop(1, count)
    def _(step):
        scatter(step).start()

    def add(step, total):
        scatter(step).wait_recv()
        return total + landed[step]

    o_ref[me] = lax.fori_loop(1, count, add, x_ref[me])

    @pl.loop(1, count)
    def _(step):
        spread(step, me).start()

    @pl.loop(1, count)
    def _(step):
        spread(step, lax.rem(me - step + count, count)).wait_recv()

    @pl.loop(1, count)
    def _(step):
        scatter(step).wait_send()
        spread(step, me).wait_send()


def sum_everywhere(terms, band_count, var_count):
    count = band_count * var_count
    rows = -(-terms.shape[0] // (8 * count)) * 8
    padded = jnp.pad(terms, ((0, rows * count - terms.shape[0]), (0, 0)))
    slots = (count, rows, terms.shape[1])
    summed = pl.pallas_call(
        functools.partial(sum_kernel, count, var_count),
        out_shape=jax.ShapeDtypeStruct(slots, jnp.float32),
        in_specs=[pl.BlockSpec(memory_space=pltpu.VMEM)],
        out_specs=pl.BlockSpec(memory_space=pltpu.VMEM),
        scratch_shapes=[pltpu.VMEM(slots, jnp.float32)]
        + [pltpu.SemaphoreType.DMA((count,)) for _ in range(4)],
        compiler_params=pltpu.CompilerParams(
            collective_id=0, has_side_effects=True, vmem_limit_bytes=32 << 20
        ),
    )(padded.reshape(slots))
    return summed.reshape(rows * count, terms.shape[1])


def token_kernel(
    bands, heads, parts,
    mix_ref, gain_ref, wq_any, wk_any, wv_any, wo_any, up_any,
    o_ref,
    wq, wk, wv, wo, up, mixes, normed, query, key, value, query_all, key_all, value_all,
    context, joined, partial, slabs,
    load, mix_out, mix_in, key_out, key_in, value_out, value_in, query_out, query_in,
    context_out, context_in, slab_out, slab_in,
):
    band = lax.axis_index("band")
    var = lax.axis_index("var")
    rows = mix_ref.shape[0]
    slab_rows = rows // parts
    head = lax.rem(band, heads)
    first = band - head

    def columns(index):
        return pl.ds(pl.multiple_of(index * HD, HD), HD)

    def lines(index, size):
        return pl.ds(pl.multiple_of(index * size, size), size)

    def remote(src, dst, out_sem, in_sem, to_band, to_var):
        return pltpu.make_async_remote_copy(
            src_ref=src, dst_ref=dst, send_sem=out_sem, recv_sem=in_sem,
            device_id=(to_band, to_var), device_id_type=MESH,
        )

    def other_band(step):
        return lax.rem(band + step, bands)

    def other_head(step):
        return lax.rem(head + step, heads)

    def other_var(step):
        return lax.rem(var + step, parts)

    def send_mix(step):
        return remote(
            mix_ref, mixes.at[step], mix_out.at[step], mix_in.at[step], band, other_var(step)
        )

    def send_rows(source, target, out_sem, in_sem, step):
        peer = other_band(step)
        return remote(
            source.at[:, columns(lax.rem(peer, heads))],
            target.at[lines(band, rows)],
            out_sem.at[step], in_sem.at[step], peer, var,
        )

    def send_query(step):
        peer = other_head(step)
        return remote(
            query.at[:, columns(peer)],
            query_all.at[lines(head, rows)],
            query_out.at[step], query_in.at[step], first + peer, var,
        )

    def send_context(peer):
        return remote(
            context.at[lines(peer, rows)],
            joined.at[:, columns(head)],
            context_out.at[peer], context_in.at[head], first + peer, var,
        )

    def take_context(owner):
        return remote(
            context.at[lines(owner, rows)],
            joined.at[:, columns(owner)],
            context_out.at[owner], context_in.at[owner], first + owner, var,
        )

    def send_slab(step):
        peer = other_var(step)
        return remote(
            partial.at[lines(peer, slab_rows)],
            slabs.at[step],
            slab_out.at[step], slab_in.at[step], band, peer,
        )

    barrier = pltpu.get_barrier_semaphore()

    @pl.loop(1, parts)
    def _(step):
        pl.semaphore_signal(
            barrier, inc=1, device_id=(band, other_var(step)), device_id_type=MESH
        )

    @pl.loop(1, bands)
    def _(step):
        pl.semaphore_signal(
            barrier, inc=1, device_id=(other_band(step), var), device_id_type=MESH
        )

    loads = [
        pltpu.make_async_copy(source, target, load.at[index])
        for index, (source, target) in enumerate(
            ((wk_any, wk), (wq_any, wq), (wv_any, wv), (wo_any, wo), (up_any, up))
        )
    ]
    for item in loads:
        item.start()
    pl.semaphore_wait(barrier, bands + parts - 2)
    for step in range(1, parts):
        send_mix(step).start()
    mixed = mix_ref[...].astype(jnp.float32)
    for step in range(1, parts):
        send_mix(step).wait_recv()
        mixed = mixed + mixes[step].astype(jnp.float32)
    scale = lax.rsqrt(jnp.mean(mixed * mixed, axis=-1, keepdims=True) + 1e-05)
    normed[...] = (mixed * scale * gain_ref[...]).astype(jnp.bfloat16)

    def project(weight):
        return jnp.dot(
            normed[...], weight[...], preferred_element_type=jnp.float32
        ).astype(jnp.bfloat16)

    loads[0].wait()
    key[...] = project(wk)

    @pl.loop(1, bands)
    def _(step):
        send_rows(key, key_all, key_out, key_in, step).start()

    loads[1].wait()
    query[...] = project(wq)

    @pl.loop(1, heads)
    def _(step):
        send_query(step).start()

    loads[2].wait()
    value[...] = project(wv)

    @pl.loop(1, bands)
    def _(step):
        send_rows(value, value_all, value_out, value_in, step).start()

    key_all[lines(band, rows), :] = key[:, columns(head)]
    value_all[lines(band, rows), :] = value[:, columns(head)]
    query_all[lines(head, rows), :] = query[:, columns(head)]

    def arrived(source, target, out_sem, in_sem, step):
        peer = lax.rem(band - step + bands, bands)
        return remote(
            source.at[:, columns(head)],
            target.at[lines(peer, rows)],
            out_sem.at[step], in_sem.at[step], other_band(step), var,
        )

    def arrived_query(step):
        peer = lax.rem(head - step + heads, heads)
        return remote(
            query.at[:, columns(head)],
            query_all.at[lines(peer, rows)],
            query_out.at[step], query_in.at[step], first + other_head(step), var,
        )

    @pl.loop(1, bands)
    def _(step):
        arrived(key, key_all, key_out, key_in, step).wait_recv()

    @pl.loop(1, heads)
    def _(step):
        arrived_query(step).wait_recv()

    group = max(1, min(heads, 256 // rows))
    size = group * rows
    for index in range(heads // group):
        scores = lax.dot_general(
            query_all[index * size : (index + 1) * size, :],
            key_all[...],
            (((1,), (1,)), ((), ())),
            preferred_element_type=jnp.float32,
        ) * (1.0 / math.sqrt(HD))
        weights = jnp.exp(scores - jnp.max(scores, axis=1, keepdims=True))
        total = jnp.sum(weights, axis=1, keepdims=True)
        probs = weights.astype(jnp.bfloat16)
        if index == 0:

            @pl.loop(1, bands)
            def _(step):
                arrived(value, value_all, value_out, value_in, step).wait_recv()

        update = jnp.dot(probs, value_all[...], preferred_element_type=jnp.float32)
        context[index * size : (index + 1) * size, :] = (update / total).astype(jnp.bfloat16)

        @pl.loop(index * group, (index + 1) * group)
        def _(peer):
            @pl.when(peer != head)
            def _():
                send_context(peer).start()

    joined[:, columns(head)] = context[lines(head, rows), :]
    loads[3].wait()
    loads[4].wait()

    @pl.loop(1, heads)
    def _(step):
        take_context(other_head(step)).wait_recv()

    partial[...] = jnp.dot(
        joined[...], wo[...], preferred_element_type=jnp.float32
    ).astype(jnp.bfloat16)
    for step in range(1, parts):
        send_slab(step).start()
    hidden = partial[lines(var, slab_rows), :].astype(jnp.float32)
    for step in range(1, parts):
        send_slab(step).wait_recv()
        hidden = hidden + slabs[step].astype(jnp.float32)
    hidden = (hidden + normed[lines(var, slab_rows), :].astype(jnp.float32)).astype(jnp.bfloat16)
    o_ref[...] = jnp.dot(hidden, up[...], preferred_element_type=jnp.float32).astype(jnp.bfloat16)

    for step in range(1, parts):
        send_mix(step).wait_send()
        send_slab(step).wait_send()

    @pl.loop(1, bands)
    def _(step):
        send_rows(key, key_all, key_out, key_in, step).wait_send()
        send_rows(value, value_all, value_out, value_in, step).wait_send()

    @pl.loop(1, heads)
    def _(step):
        send_query(step).wait_send()
        send_context(other_head(step)).wait_send()


def token_stage(own_mix, agg_gain, wq, wk, wv, wo, w_up, bands, parts):
    rows = own_mix.shape[0]
    wide = wq.shape[1]
    heads = wide // HD
    fine = w_up.shape[1]

    def half(*shape):
        return pltpu.VMEM(shape, jnp.bfloat16)

    def flags(count):
        return pltpu.SemaphoreType.DMA((count,))

    vmem = pl.BlockSpec(memory_space=pltpu.VMEM)
    return pl.pallas_call(
        functools.partial(token_kernel, bands, heads, parts),
        out_shape=jax.ShapeDtypeStruct((rows // parts, fine), jnp.bfloat16),
        in_specs=[vmem, vmem] + [pl.BlockSpec(memory_space=pl.ANY)] * 5,
        out_specs=vmem,
        scratch_shapes=[
            half(D, wide), half(D, wide), half(D, wide), half(wide, D), half(D, fine),
            half(parts, rows, D), half(rows, D),
            half(rows, wide), half(rows, wide), half(rows, wide),
            half(heads * rows, HD), half(bands * rows, HD), half(bands * rows, HD),
            half(heads * rows, HD), half(rows, wide), half(rows, D),
            half(parts, rows // parts, D),
            flags(5), flags(parts), flags(parts), flags(bands), flags(bands), flags(bands),
            flags(bands), flags(heads), flags(heads), flags(heads), flags(heads),
            flags(parts), flags(parts),
        ],
        compiler_params=pltpu.CompilerParams(
            collective_id=1, has_side_effects=True, vmem_limit_bytes=56 << 20
        ),
    )(own_mix, agg_gain[None], wq, wk, wv, wo, w_up)


def on_device(
    patches, w_embed, var_bias, agg_gain, wq, wk, wv, wo, w_up, conv1, bias1, conv2, cotangent
):
    var_count = lax.axis_size("var")
    band_count = lax.axis_size("band")
    var_local, lat_dev, lon_all, patch_len = patches.shape
    lon_dev = lon_all // var_count
    flattened = jnp.transpose(patches, (1, 2, 0, 3)).reshape(
        lat_dev * lon_all, var_local * patch_len
    )
    partial_mix = jnp.dot(
        flattened, w_embed.reshape(var_local * patch_len, D), preferred_element_type=jnp.float32
    )
    own_mix = (partial_mix + jnp.sum(var_bias, axis=0)).astype(jnp.bfloat16)
    token_rows = jnp.transpose(
        own_mix.reshape(lat_dev, var_count, lon_dev, D), (1, 0, 2, 3)
    ).reshape(-1, D)
    upsampled = token_stage(
        token_rows, agg_gain, wq, wk, wv, wo, w_up, band_count, var_count
    )
    height = lat_dev * R
    width = lon_dev * R
    upsampled = jnp.transpose(
        upsampled.reshape(lat_dev, lon_dev, R, R, C), (0, 2, 4, 1, 3)
    ).reshape(height, C, width)
    bias_cols = bias1[None, :, None]
    widened = with_halo(upsampled, (("band", 0), ("var", 2)), 2)
    pre_wide = conv_padded(widened, conv1, height + 2, width + 2) + bias_cols
    row_ids = lax.axis_index("band") * height + jnp.arange(height + 2) - 1
    col_ids = lax.axis_index("var") * width + jnp.arange(width + 2) - 1
    rows_inside = (row_ids >= 0) & (row_ids < height * band_count)
    cols_inside = (col_ids >= 0) & (col_ids < width * var_count)
    inside = rows_inside[:, None, None] & cols_inside[None, None, :]
    active_pad = jnp.where(inside, jax.nn.gelu(pre_wide), 0.0).astype(jnp.bfloat16)
    fine_pad = widened[1:-1, :, 1:-1]
    pre = pre_wide[1:-1, :, 1:-1]
    field_out = (
        conv_padded(active_pad, conv2, height, width) + upsampled.astype(jnp.float32)
    ).astype(jnp.bfloat16)
    cotangent_pad = gradient_rim(cotangent)
    d_active = conv_padded(cotangent_pad, flipped(conv2), height, width)
    d_pre = jax.vjp(jax.nn.gelu, pre)[1](d_active)[0].astype(jnp.bfloat16)
    d_pre_pad = gradient_rim(d_pre)
    grad_fine = (
        cotangent.astype(jnp.float32) + conv_padded(d_pre_pad, flipped(conv1), height, width)
    ).astype(jnp.bfloat16)
    factor = 1.0 / math.sqrt(height * band_count * width * var_count)
    first_terms = weight_grad(fine_pad, d_pre).reshape(9 * C, C) * factor
    second_terms = weight_grad(active_pad, cotangent).reshape(9 * C, C) * factor
    bias_terms = jnp.sum(d_pre.astype(jnp.float32), axis=(0, 2)) * factor
    terms = jnp.concatenate([first_terms, second_terms], axis=1)
    bias_row = jnp.pad(bias_terms, (0, C))[None]
    summed = sum_everywhere(jnp.concatenate([terms, bias_row], axis=0), band_count, var_count)
    grad_conv1 = summed[: 9 * C, :C].reshape(9, C, C)
    grad_conv2 = summed[: 9 * C, C:].reshape(9, C, C)
    grad_bias = summed[9 * C, :C]
    return (field_out, grad_fine, grad_conv1, grad_conv2, grad_bias)


def solution(mesh):
    in_specs = (
        P("var", "band", None, None),
        P("var", None, None),
        P("var", None),
        P(),
        P(None, "var"),
        P(None, "var"),
        P(None, "var"),
        P("var", None),
        P(),
        P(),
        P(),
        P(),
        P("band", None, "var"),
    )
    out_specs = (P("band", None, "var"), P("band", None, "var"), P(), P(), P())
    return jax.shard_map(
        on_device, mesh=mesh, in_specs=in_specs, out_specs=out_specs, check_vma=False
    )
```

```python
import functools
import math

import jax
import jax.numpy as jnp
from jax import lax
from jax.experimental import pallas as pl
from jax.experimental.pallas import tpu as pltpu
from jax.sharding import PartitionSpec as P

MESH = pl.DeviceIdType.MESH

D = 2048
HD = 128
C = 64
R = 4


def tap_stack(padded, height, width):
    pieces = [
        padded[row_tap : row_tap + height, :, col_tap : col_tap + width]
        for row_tap in range(3)
        for col_tap in range(3)
    ]
    return jnp.concatenate(pieces, axis=1)


def conv_padded(padded, weight, height, width):
    stacked = tap_stack(padded, height, width)
    return jnp.einsum(
        "ykx,ko->yox",
        stacked,
        weight.reshape(-1, weight.shape[2]),
        preferred_element_type=jnp.float32,
    )


def flipped(weight):
    return jnp.transpose(weight[::-1], (0, 2, 1))


def weight_grad(padded, grads):
    stacked = tap_stack(padded, grads.shape[0], grads.shape[2])
    summed = jnp.einsum("ykx,yox->ko", stacked, grads, preferred_element_type=jnp.float32)
    return summed.reshape(9, padded.shape[1], grads.shape[1])


SIDES = [(down, right) for down in (-1, 0, 1) for right in (-1, 0, 1) if down or right]


def present(bands, parts, down, right):
    band = lax.axis_index("band") + down
    var = lax.axis_index("var") + right
    return (band >= 0) & (band < bands) & (var >= 0) & (var < parts)


def to_sides(bands, parts, pieces, out_sem, in_sem):
    copies = []
    for index, (down, right) in enumerate(SIDES):
        source, target = pieces(down, right)
        copies.append(
            pltpu.make_async_remote_copy(
                src_ref=source,
                dst_ref=target,
                send_sem=out_sem.at[index],
                recv_sem=in_sem.at[index],
                device_id=(lax.axis_index("band") + down, lax.axis_index("var") + right),
                device_id_type=MESH,
            )
        )

    def start():
        for copy, (down, right) in zip(copies, SIDES):
            pl.when(present(bands, parts, down, right))(copy.start)

    def take():
        for copy, (down, right) in zip(copies, SIDES):
            pl.when(present(bands, parts, -down, -right))(copy.wait_recv)

    def finish():
        for copy, (down, right) in zip(copies, SIDES):
            pl.when(present(bands, parts, down, right))(copy.wait_send)

    return start, take, finish


def rim_pieces(field, rim):
    height = field.shape[0]

    def pieces(down, right):
        take, put = {-1: (0, height + 1), 0: (0, 1), 1: (height - 1, 0)}[down]
        size = 1 if down else height
        return field.at[pl.ds(take, size)], rim.at[1 - right, pl.ds(put, size)]

    return pieces


def rim_shape(field):
    return jax.ShapeDtypeStruct((3, field.shape[0] + 2) + field.shape[1:], field.dtype)


def padded_from(rim):
    return jnp.concatenate([rim[0, :, :, -1:], rim[1], rim[2, :, :, :1]], axis=2)


def sum_kernel(
    count, var_count, x_ref, field_ref, o_ref, rim_ref,
    landed, send1, recv1, send2, recv2, rim_out, rim_in,
):
    rim_ref[...] = jnp.zeros_like(rim_ref)
    rim_start, rim_take, rim_finish = to_sides(
        count // var_count, var_count, rim_pieces(field_ref, rim_ref), rim_out, rim_in
    )
    me = lax.axis_index("band") * var_count + lax.axis_index("var")

    def place(device):
        return (lax.div(device, var_count), lax.rem(device, var_count))

    def scatter(step):
        peer = lax.rem(me + step, count)
        return pltpu.make_async_remote_copy(
            src_ref=x_ref.at[peer],
            dst_ref=landed.at[step],
            send_sem=send1.at[step],
            recv_sem=recv1.at[step],
            device_id=place(peer),
            device_id_type=MESH,
        )

    def spread(step, owner):
        return pltpu.make_async_remote_copy(
            src_ref=o_ref.at[owner],
            dst_ref=o_ref.at[owner],
            send_sem=send2.at[step],
            recv_sem=recv2.at[step],
            device_id=place(lax.rem(me + step, count)),
            device_id_type=MESH,
        )

    barrier = pltpu.get_barrier_semaphore()

    @pl.loop(1, count)
    def _(step):
        pl.semaphore_signal(
            barrier, inc=1, device_id=place(lax.rem(me + step, count)), device_id_type=MESH
        )

    pl.semaphore_wait(barrier, count - 1)
    rim_start()
    rim_ref[1, 1 : field_ref.shape[0] + 1] = field_ref[...]

    @pl.loop(1, count)
    def _(step):
        scatter(step).start()

    def add(step, total):
        scatter(step).wait_recv()
        return total + landed[step]

    o_ref[me] = lax.fori_loop(1, count, add, x_ref[me])

    @pl.loop(1, count)
    def _(step):
        spread(step, me).start()

    @pl.loop(1, count)
    def _(step):
        spread(step, lax.rem(me - step + count, count)).wait_recv()

    @pl.loop(1, count)
    def _(step):
        scatter(step).wait_send()
        spread(step, me).wait_send()

    rim_take()
    rim_finish()


def sum_everywhere(terms, field, band_count, var_count):
    count = band_count * var_count
    rows = -(-terms.shape[0] // (8 * count)) * 8
    padded = jnp.pad(terms, ((0, rows * count - terms.shape[0]), (0, 0)))
    slots = (count, rows, terms.shape[1])
    vmem = pl.BlockSpec(memory_space=pltpu.VMEM)
    summed, rim = pl.pallas_call(
        functools.partial(sum_kernel, count, var_count),
        out_shape=(jax.ShapeDtypeStruct(slots, jnp.float32), rim_shape(field)),
        in_specs=[vmem, vmem],
        out_specs=(vmem, vmem),
        scratch_shapes=[pltpu.VMEM(slots, jnp.float32)]
        + [pltpu.SemaphoreType.DMA((count,)) for _ in range(4)]
        + [pltpu.SemaphoreType.DMA((8,)) for _ in range(2)],
        compiler_params=pltpu.CompilerParams(
            collective_id=0, has_side_effects=True, vmem_limit_bytes=32 << 20
        ),
    )(padded.reshape(slots), field)
    return summed.reshape(rows * count, terms.shape[1]), padded_from(rim)


def token_kernel(
    bands, heads, parts,
    mix_ref, gain_ref, field_ref, wq_any, wk_any, wv_any, wo_any, up_any,
    o_ref, rim_ref,
    wq, wk, wv, wo, up, mixes, normed, query, key, value, query_all, key_all, value_all,
    context, joined, partial, slabs,
    load, mix_out, mix_in, key_out, key_in, value_out, value_in, query_out, query_in,
    context_out, context_in, slab_out, slab_in, rim_out, rim_in, fine_out, fine_in,
):
    o_ref[...] = jnp.zeros_like(o_ref)
    rim_ref[...] = jnp.zeros_like(rim_ref)
    rim_start, rim_take, rim_finish = to_sides(
        bands, parts, rim_pieces(field_ref, rim_ref), rim_out, rim_in
    )
    band = lax.axis_index("band")
    var = lax.axis_index("var")
    rows = mix_ref.shape[0]
    slab_rows = rows // parts
    head = lax.rem(band, heads)
    first = band - head

    def columns(index):
        return pl.ds(pl.multiple_of(index * HD, HD), HD)

    def lines(index, size):
        return pl.ds(pl.multiple_of(index * size, size), size)

    def remote(src, dst, out_sem, in_sem, to_band, to_var):
        return pltpu.make_async_remote_copy(
            src_ref=src, dst_ref=dst, send_sem=out_sem, recv_sem=in_sem,
            device_id=(to_band, to_var), device_id_type=MESH,
        )

    def other_band(step):
        return lax.rem(band + step, bands)

    def other_head(step):
        return lax.rem(head + step, heads)

    def other_var(step):
        return lax.rem(var + step, parts)

    def send_mix(step):
        return remote(
            mix_ref, mixes.at[step], mix_out.at[step], mix_in.at[step], band, other_var(step)
        )

    def send_rows(source, target, out_sem, in_sem, step):
        peer = other_band(step)
        return remote(
            source.at[:, columns(lax.rem(peer, heads))],
            target.at[lines(band, rows)],
            out_sem.at[step], in_sem.at[step], peer, var,
        )

    def send_query(step):
        peer = other_head(step)
        return remote(
            query.at[:, columns(peer)],
            query_all.at[lines(head, rows)],
            query_out.at[step], query_in.at[step], first + peer, var,
        )

    def send_context(peer):
        return remote(
            context.at[lines(peer, rows)],
            joined.at[:, columns(head)],
            context_out.at[peer], context_in.at[head], first + peer, var,
        )

    def take_context(owner):
        return remote(
            context.at[lines(owner, rows)],
            joined.at[:, columns(owner)],
            context_out.at[owner], context_in.at[owner], first + owner, var,
        )

    def send_slab(step):
        peer = other_var(step)
        return remote(
            partial.at[lines(peer, slab_rows)],
            slabs.at[step],
            slab_out.at[step], slab_in.at[step], band, peer,
        )

    middle = up_any.shape[1] // 2

    def fine_pieces(down, right):
        take, put = {-1: (1, 3), 0: (1, 1), 1: (2, 0)}[down]
        size = middle if down else 2 * middle
        start, land, length = {
            -1: (16, 16 + slab_rows, 16),
            0: (16, 16, slab_rows),
            1: (slab_rows, 0, 16),
        }[right]
        return (
            o_ref.at[pl.ds(start, length), pl.ds(take * middle, size)],
            o_ref.at[pl.ds(land, length), pl.ds(put * middle, size)],
        )

    fine_start, fine_take, fine_finish = to_sides(bands, parts, fine_pieces, fine_out, fine_in)
    barrier = pltpu.get_barrier_semaphore()
    corners = 0
    for down, right in SIDES:
        if down and right:
            there = present(bands, parts, down, right)
            corners = corners + there.astype(jnp.int32)

            @pl.when(there)
            def _():
                pl.semaphore_signal(
                    barrier, inc=1, device_id=(band + down, var + right), device_id_type=MESH
                )

    @pl.loop(1, parts)
    def _(step):
        pl.semaphore_signal(
            barrier, inc=1, device_id=(band, other_var(step)), device_id_type=MESH
        )

    @pl.loop(1, bands)
    def _(step):
        pl.semaphore_signal(
            barrier, inc=1, device_id=(other_band(step), var), device_id_type=MESH
        )

    loads = [
        pltpu.make_async_copy(source, target, load.at[index])
        for index, (source, target) in enumerate(
            ((wk_any, wk), (wq_any, wq), (wv_any, wv), (wo_any, wo), (up_any, up))
        )
    ]
    for item in loads:
        item.start()
    pl.semaphore_wait(barrier, bands + parts - 2 + corners)
    for step in range(1, parts):
        send_mix(step).start()
    rim_start()
    rim_ref[1, 1 : field_ref.shape[0] + 1] = field_ref[...]
    mixed = mix_ref[...].astype(jnp.float32)
    for step in range(1, parts):
        send_mix(step).wait_recv()
        mixed = mixed + mixes[step].astype(jnp.float32)
    scale = lax.rsqrt(jnp.mean(mixed * mixed, axis=-1, keepdims=True) + 1e-05)
    normed[...] = (mixed * scale * gain_ref[...]).astype(jnp.bfloat16)

    def project(weight):
        return jnp.dot(
            normed[...], weight[...], preferred_element_type=jnp.float32
        ).astype(jnp.bfloat16)

    loads[0].wait()
    key[...] = project(wk)

    @pl.loop(1, bands)
    def _(step):
        send_rows(key, key_all, key_out, key_in, step).start()

    loads[1].wait()
    query[...] = project(wq)

    @pl.loop(1, heads)
    def _(step):
        send_query(step).start()

    loads[2].wait()
    value[...] = project(wv)

    @pl.loop(1, bands)
    def _(step):
        send_rows(value, value_all, value_out, value_in, step).start()

    key_all[lines(band, rows), :] = key[:, columns(head)]
    value_all[lines(band, rows), :] = value[:, columns(head)]
    query_all[lines(head, rows), :] = query[:, columns(head)]

    def arrived(source, target, out_sem, in_sem, step):
        peer = lax.rem(band - step + bands, bands)
        return remote(
            source.at[:, columns(head)],
            target.at[lines(peer, rows)],
            out_sem.at[step], in_sem.at[step], other_band(step), var,
        )

    def arrived_query(step):
        peer = lax.rem(head - step + heads, heads)
        return remote(
            query.at[:, columns(head)],
            query_all.at[lines(peer, rows)],
            query_out.at[step], query_in.at[step], first + other_head(step), var,
        )

    @pl.loop(1, bands)
    def _(step):
        arrived(key, key_all, key_out, key_in, step).wait_recv()

    @pl.loop(1, heads)
    def _(step):
        arrived_query(step).wait_recv()

    group = max(1, min(heads, 256 // rows))
    size = group * rows
    for index in range(heads // group):
        scores = lax.dot_general(
            query_all[index * size : (index + 1) * size, :],
            key_all[...],
            (((1,), (1,)), ((), ())),
            preferred_element_type=jnp.float32,
        ) * (1.0 / math.sqrt(HD))
        weights = jnp.exp(scores - jnp.max(scores, axis=1, keepdims=True))
        total = jnp.sum(weights, axis=1, keepdims=True)
        probs = weights.astype(jnp.bfloat16)
        if index == 0:

            @pl.loop(1, bands)
            def _(step):
                arrived(value, value_all, value_out, value_in, step).wait_recv()

        update = jnp.dot(probs, value_all[...], preferred_element_type=jnp.float32)
        context[index * size : (index + 1) * size, :] = (update / total).astype(jnp.bfloat16)

        @pl.loop(index * group, (index + 1) * group)
        def _(peer):
            @pl.when(peer != head)
            def _():
                send_context(peer).start()

    joined[:, columns(head)] = context[lines(head, rows), :]
    loads[3].wait()
    loads[4].wait()

    @pl.loop(1, heads)
    def _(step):
        take_context(other_head(step)).wait_recv()

    partial[...] = jnp.dot(
        joined[...], wo[...], preferred_element_type=jnp.float32
    ).astype(jnp.bfloat16)
    for step in range(1, parts):
        send_slab(step).start()
    hidden = partial[lines(var, slab_rows), :].astype(jnp.float32)
    for step in range(1, parts):
        send_slab(step).wait_recv()
        hidden = hidden + slabs[step].astype(jnp.float32)
    hidden = (hidden + normed[lines(var, slab_rows), :].astype(jnp.float32)).astype(jnp.bfloat16)
    o_ref[16 : 16 + slab_rows, middle : 3 * middle] = jnp.dot(
        hidden, up[...], preferred_element_type=jnp.float32
    ).astype(jnp.bfloat16)
    fine_start()
    rim_take()
    rim_finish()

    for step in range(1, parts):
        send_mix(step).wait_send()
        send_slab(step).wait_send()

    @pl.loop(1, bands)
    def _(step):
        send_rows(key, key_all, key_out, key_in, step).wait_send()
        send_rows(value, value_all, value_out, value_in, step).wait_send()

    @pl.loop(1, heads)
    def _(step):
        send_query(step).wait_send()
        send_context(other_head(step)).wait_send()

    fine_take()
    fine_finish()


def token_stage(own_mix, agg_gain, field, wq, wk, wv, wo, w_up, bands, parts):
    rows = own_mix.shape[0]
    wide = wq.shape[1]
    heads = wide // HD
    fine = w_up.shape[1]

    def half(*shape):
        return pltpu.VMEM(shape, jnp.bfloat16)

    def flags(count):
        return pltpu.SemaphoreType.DMA((count,))

    vmem = pl.BlockSpec(memory_space=pltpu.VMEM)
    return pl.pallas_call(
        functools.partial(token_kernel, bands, heads, parts),
        out_shape=(
            jax.ShapeDtypeStruct((rows // parts + 32, 2 * fine), jnp.bfloat16),
            rim_shape(field),
        ),
        in_specs=[vmem] * 3 + [pl.BlockSpec(memory_space=pl.ANY)] * 5,
        out_specs=(vmem, vmem),
        scratch_shapes=[
            half(D, wide), half(D, wide), half(D, wide), half(wide, D), half(D, fine),
            half(parts, rows, D), half(rows, D),
            half(rows, wide), half(rows, wide), half(rows, wide),
            half(heads * rows, HD), half(bands * rows, HD), half(bands * rows, HD),
            half(heads * rows, HD), half(rows, wide), half(rows, D),
            half(parts, rows // parts, D),
            flags(5), flags(parts), flags(parts), flags(bands), flags(bands), flags(bands),
            flags(bands), flags(heads), flags(heads), flags(heads), flags(heads),
            flags(parts), flags(parts), flags(8), flags(8), flags(8), flags(8),
        ],
        compiler_params=pltpu.CompilerParams(
            collective_id=1, has_side_effects=True, vmem_limit_bytes=56 << 20
        ),
    )(own_mix, agg_gain[None], field, wq, wk, wv, wo, w_up)


def on_device(
    patches, w_embed, var_bias, agg_gain, wq, wk, wv, wo, w_up, conv1, bias1, conv2, cotangent
):
    var_count = lax.axis_size("var")
    band_count = lax.axis_size("band")
    var_local, lat_dev, lon_all, patch_len = patches.shape
    lon_dev = lon_all // var_count
    flattened = jnp.transpose(patches, (1, 2, 0, 3)).reshape(
        lat_dev * lon_all, var_local * patch_len
    )
    partial_mix = jnp.dot(
        flattened, w_embed.reshape(var_local * patch_len, D), preferred_element_type=jnp.float32
    )
    own_mix = (partial_mix + jnp.sum(var_bias, axis=0)).astype(jnp.bfloat16)
    token_rows = jnp.transpose(
        own_mix.reshape(lat_dev, var_count, lon_dev, D), (1, 0, 2, 3)
    ).reshape(-1, D)
    around, rim = token_stage(
        token_rows, agg_gain, cotangent, wq, wk, wv, wo, w_up, band_count, var_count
    )
    height = lat_dev * R
    width = lon_dev * R
    fine_wide = jnp.transpose(
        around.reshape(lon_dev + 32, 2 * R, R, C), (1, 3, 0, 2)
    ).reshape(2 * R, C, width + 32 * R)
    widened = fine_wide[:, :, 16 * R - 2 : 16 * R + width + 2]
    upsampled = fine_wide[2 : 2 + height, :, 16 * R : 16 * R + width]
    bias_cols = bias1[None, :, None]
    pre_wide = conv_padded(widened, conv1, height + 2, width + 2) + bias_cols
    row_ids = lax.axis_index("band") * height + jnp.arange(height + 2) - 1
    col_ids = lax.axis_index("var") * width + jnp.arange(width + 2) - 1
    rows_inside = (row_ids >= 0) & (row_ids < height * band_count)
    cols_inside = (col_ids >= 0) & (col_ids < width * var_count)
    inside = rows_inside[:, None, None] & cols_inside[None, None, :]
    active_pad = jnp.where(inside, jax.nn.gelu(pre_wide), 0.0).astype(jnp.bfloat16)
    fine_pad = widened[1:-1, :, 1:-1]
    pre = pre_wide[1:-1, :, 1:-1]
    field_out = (
        conv_padded(active_pad, conv2, height, width) + upsampled.astype(jnp.float32)
    ).astype(jnp.bfloat16)
    cotangent_pad = padded_from(rim)
    d_active = conv_padded(cotangent_pad, flipped(conv2), height, width)
    d_pre = jax.vjp(jax.nn.gelu, pre)[1](d_active)[0].astype(jnp.bfloat16)
    factor = 1.0 / math.sqrt(height * band_count * width * var_count)
    first_terms = weight_grad(fine_pad, d_pre).reshape(9 * C, C) * factor
    second_terms = weight_grad(active_pad, cotangent).reshape(9 * C, C) * factor
    bias_terms = jnp.sum(d_pre.astype(jnp.float32), axis=(0, 2)) * factor
    terms = jnp.concatenate([first_terms, second_terms], axis=1)
    bias_row = jnp.pad(bias_terms, (0, C))[None]
    summed, d_pre_pad = sum_everywhere(
        jnp.concatenate([terms, bias_row], axis=0), d_pre, band_count, var_count
    )
    grad_fine = (
        cotangent.astype(jnp.float32) + conv_padded(d_pre_pad, flipped(conv1), height, width)
    ).astype(jnp.bfloat16)
    grad_conv1 = summed[: 9 * C, :C].reshape(9, C, C)
    grad_conv2 = summed[: 9 * C, C:].reshape(9, C, C)
    grad_bias = summed[9 * C, :C]
    return (field_out, grad_fine, grad_conv1, grad_conv2, grad_bias)


def solution(mesh):
    in_specs = (
        P("var", "band", None, None),
        P("var", None, None),
        P("var", None),
        P(),
        P(None, "var"),
        P(None, "var"),
        P(None, "var"),
        P("var", None),
        P(),
        P(),
        P(),
        P(),
        P("band", None, "var"),
    )
    out_specs = (P("band", None, "var"), P("band", None, "var"), P(), P(), P())
    return jax.shard_map(
        on_device, mesh=mesh, in_specs=in_specs, out_specs=out_specs, check_vma=False
    )
```

```python
import functools
import math

import jax
import jax.numpy as jnp
from jax import lax
from jax.experimental import pallas as pl
from jax.experimental.pallas import tpu as pltpu
from jax.sharding import PartitionSpec as P

MESH = pl.DeviceIdType.MESH

D = 2048
HD = 128
C = 64
R = 4


def tap_stack(padded, height, width):
    pieces = [
        padded[row_tap : row_tap + height, :, col_tap : col_tap + width]
        for row_tap in range(3)
        for col_tap in range(3)
    ]
    return jnp.concatenate(pieces, axis=1)


def conv_padded(padded, weight, height, width):
    stacked = tap_stack(padded, height, width)
    return jnp.einsum(
        "ykx,ko->yox",
        stacked,
        weight.reshape(-1, weight.shape[2]),
        preferred_element_type=jnp.float32,
    )


def flipped(weight):
    return jnp.transpose(weight[::-1], (0, 2, 1))


def weight_grad(padded, grads):
    stacked = tap_stack(padded, grads.shape[0], grads.shape[2])
    summed = jnp.einsum("ykx,yox->ko", stacked, grads, preferred_element_type=jnp.float32)
    return summed.reshape(9, padded.shape[1], grads.shape[1])


SIDES = [(down, right) for down in (-1, 0, 1) for right in (-1, 0, 1) if down or right]


def present(bands, parts, down, right):
    band = lax.axis_index("band") + down
    var = lax.axis_index("var") + right
    return (band >= 0) & (band < bands) & (var >= 0) & (var < parts)


def to_sides(bands, parts, pieces, out_sem, in_sem):
    copies = []
    for index, (down, right) in enumerate(SIDES):
        source, target = pieces(down, right)
        copies.append(
            pltpu.make_async_remote_copy(
                src_ref=source,
                dst_ref=target,
                send_sem=out_sem.at[index],
                recv_sem=in_sem.at[index],
                device_id=(lax.axis_index("band") + down, lax.axis_index("var") + right),
                device_id_type=MESH,
            )
        )

    def start():
        for copy, (down, right) in zip(copies, SIDES):
            pl.when(present(bands, parts, down, right))(copy.start)

    def take():
        for copy, (down, right) in zip(copies, SIDES):
            pl.when(present(bands, parts, -down, -right))(copy.wait_recv)

    def finish():
        for copy, (down, right) in zip(copies, SIDES):
            pl.when(present(bands, parts, down, right))(copy.wait_send)

    return start, take, finish


def rim_pieces(field, rim):
    height = field.shape[0]

    def pieces(down, right):
        take, put = {-1: (0, height + 1), 0: (0, 1), 1: (height - 1, 0)}[down]
        size = 1 if down else height
        return field.at[pl.ds(take, size)], rim.at[1 - right, pl.ds(put, size)]

    return pieces


def rim_shape(field):
    return jax.ShapeDtypeStruct((3, field.shape[0] + 2) + field.shape[1:], field.dtype)


def padded_from(rim):
    return jnp.concatenate([rim[0, :, :, -1:], rim[1], rim[2, :, :, :1]], axis=2)


def sum_kernel(
    count, var_count, x_ref, field_ref, o_ref, rim_ref,
    paired, sums, landed, pair_out, pair_in, send1, recv1, send2, recv2, rim_out, rim_in,
):
    rim_ref[...] = jnp.zeros_like(rim_ref)
    rim_start, rim_take, rim_finish = to_sides(
        count // var_count, var_count, rim_pieces(field_ref, rim_ref), rim_out, rim_in
    )
    me = lax.axis_index("band") * var_count + lax.axis_index("var")

    def place(device):
        return (lax.div(device, var_count), lax.rem(device, var_count))

    half = count // 2
    band = lax.axis_index("band")
    core = lax.rem(band, 2)
    group = lax.div(band, 2) * var_count + lax.axis_index("var")
    mine = core * half

    def in_group(index):
        return (lax.div(index, var_count) * 2 + core, lax.rem(index, var_count))

    def remote(source, target, out_sem, in_sem, device):
        return pltpu.make_async_remote_copy(
            src_ref=source,
            dst_ref=target,
            send_sem=out_sem,
            recv_sem=in_sem,
            device_id=device,
            device_id_type=MESH,
        )

    partner = (band + 1 - 2 * core, lax.axis_index("var"))

    def give_half():
        theirs = pl.ds((1 - core) * half, half)
        return remote(x_ref.at[theirs], paired, pair_out.at[0], pair_in.at[0], partner)

    def share_half(owner):
        part = pl.ds(owner * half, half)
        return remote(o_ref.at[part], o_ref.at[part], pair_out.at[1], pair_in.at[1], partner)

    def scatter(step):
        peer = lax.rem(group + step, half)
        return remote(
            sums.at[peer], landed.at[step], send1.at[step], recv1.at[step], in_group(peer)
        )

    def spread(step, owner):
        peer = lax.rem(group + step, half)
        slot = o_ref.at[mine + owner]
        return remote(slot, slot, send2.at[step], recv2.at[step], in_group(peer))

    barrier = pltpu.get_barrier_semaphore()

    @pl.loop(1, count)
    def _(step):
        pl.semaphore_signal(
            barrier, inc=1, device_id=place(lax.rem(me + step, count)), device_id_type=MESH
        )

    pl.semaphore_wait(barrier, count - 1)
    give_half().start()
    rim_start()
    rim_ref[1, 1 : field_ref.shape[0] + 1] = field_ref[...]

    give_half().wait_recv()

    @pl.loop(0, half)
    def _(index):
        sums[index] = x_ref[mine + index] + paired[index]

    @pl.loop(1, half)
    def _(step):
        scatter(step).start()

    def add(step, total):
        scatter(step).wait_recv()
        return total + landed[step]

    o_ref[mine + group] = lax.fori_loop(1, half, add, sums[group])

    @pl.loop(1, half)
    def _(step):
        spread(step, group).start()

    @pl.loop(1, half)
    def _(step):
        spread(step, lax.rem(group - step + half, half)).wait_recv()

    share_half(core).start()
    give_half().wait_send()

    @pl.loop(1, half)
    def _(step):
        scatter(step).wait_send()
        spread(step, group).wait_send()

    share_half(1 - core).wait_recv()
    share_half(core).wait_send()
    rim_take()
    rim_finish()


def sum_everywhere(terms, field, band_count, var_count):
    count = band_count * var_count
    rows = -(-terms.shape[0] // (8 * count)) * 8
    padded = jnp.pad(terms, ((0, rows * count - terms.shape[0]), (0, 0)))
    slots = (count, rows, terms.shape[1])
    vmem = pl.BlockSpec(memory_space=pltpu.VMEM)
    summed, rim = pl.pallas_call(
        functools.partial(sum_kernel, count, var_count),
        out_shape=(jax.ShapeDtypeStruct(slots, jnp.float32), rim_shape(field)),
        in_specs=[vmem, vmem],
        out_specs=(vmem, vmem),
        scratch_shapes=[pltpu.VMEM((count // 2,) + slots[1:], jnp.float32) for _ in range(3)]
        + [pltpu.SemaphoreType.DMA((2,)) for _ in range(2)]
        + [pltpu.SemaphoreType.DMA((count // 2,)) for _ in range(4)]
        + [pltpu.SemaphoreType.DMA((8,)) for _ in range(2)],
        compiler_params=pltpu.CompilerParams(
            collective_id=0, has_side_effects=True, vmem_limit_bytes=32 << 20
        ),
    )(padded.reshape(slots), field)
    return summed.reshape(rows * count, terms.shape[1]), padded_from(rim)


def token_kernel(
    bands, heads, parts,
    mix_ref, gain_ref, field_ref, wq_any, wk_any, wv_any, wo_any, up_any,
    o_ref, rim_ref,
    wq, wk, wv, wo, up, mixes, normed, query, key, value, query_all, key_all, value_all,
    context, joined, partial, slabs,
    load, mix_out, mix_in, key_out, key_in, value_out, value_in, query_out, query_in,
    context_out, context_in, slab_out, slab_in, rim_out, rim_in, fine_out, fine_in,
):
    o_ref[...] = jnp.zeros_like(o_ref)
    rim_ref[...] = jnp.zeros_like(rim_ref)
    rim_start, rim_take, rim_finish = to_sides(
        bands, parts, rim_pieces(field_ref, rim_ref), rim_out, rim_in
    )
    band = lax.axis_index("band")
    var = lax.axis_index("var")
    rows = mix_ref.shape[0]
    slab_rows = rows // parts
    head = lax.rem(band, heads)
    first = band - head

    def columns(index):
        return pl.ds(pl.multiple_of(index * HD, HD), HD)

    def lines(index, size):
        return pl.ds(pl.multiple_of(index * size, size), size)

    def remote(src, dst, out_sem, in_sem, to_band, to_var):
        return pltpu.make_async_remote_copy(
            src_ref=src, dst_ref=dst, send_sem=out_sem, recv_sem=in_sem,
            device_id=(to_band, to_var), device_id_type=MESH,
        )

    def other_band(step):
        return lax.rem(band + step, bands)

    def other_head(step):
        return lax.rem(head + step, heads)

    def other_var(step):
        return lax.rem(var + step, parts)

    def send_mix(step):
        return remote(
            mix_ref, mixes.at[step], mix_out.at[step], mix_in.at[step], band, other_var(step)
        )

    def send_rows(source, target, out_sem, in_sem, step):
        peer = other_band(step)
        return remote(
            source.at[:, columns(lax.rem(peer, heads))],
            target.at[lines(band, rows)],
            out_sem.at[step], in_sem.at[step], peer, var,
        )

    def send_query(step):
        peer = other_head(step)
        return remote(
            query.at[:, columns(peer)],
            query_all.at[lines(head, rows)],
            query_out.at[step], query_in.at[step], first + peer, var,
        )

    def send_context(peer):
        return remote(
            context.at[lines(peer, rows)],
            joined.at[:, columns(head)],
            context_out.at[peer], context_in.at[head], first + peer, var,
        )

    def take_context(owner):
        return remote(
            context.at[lines(owner, rows)],
            joined.at[:, columns(owner)],
            context_out.at[owner], context_in.at[owner], first + owner, var,
        )

    def send_slab(step):
        peer = other_var(step)
        return remote(
            partial.at[lines(peer, slab_rows)],
            slabs.at[step],
            slab_out.at[step], slab_in.at[step], band, peer,
        )

    middle = up_any.shape[1] // 2

    def fine_pieces(down, right):
        take, put = {-1: (1, 3), 0: (1, 1), 1: (2, 0)}[down]
        size = middle if down else 2 * middle
        start, land, length = {
            -1: (16, 16 + slab_rows, 16),
            0: (16, 16, slab_rows),
            1: (slab_rows, 0, 16),
        }[right]
        return (
            o_ref.at[pl.ds(start, length), pl.ds(take * middle, size)],
            o_ref.at[pl.ds(land, length), pl.ds(put * middle, size)],
        )

    fine_start, fine_take, fine_finish = to_sides(bands, parts, fine_pieces, fine_out, fine_in)
    barrier = pltpu.get_barrier_semaphore()
    corners = 0
    for down, right in SIDES:
        if down and right:
            there = present(bands, parts, down, right)
            corners = corners + there.astype(jnp.int32)

            @pl.when(there)
            def _():
                pl.semaphore_signal(
                    barrier, inc=1, device_id=(band + down, var + right), device_id_type=MESH
                )

    @pl.loop(1, parts)
    def _(step):
        pl.semaphore_signal(
            barrier, inc=1, device_id=(band, other_var(step)), device_id_type=MESH
        )

    @pl.loop(1, bands)
    def _(step):
        pl.semaphore_signal(
            barrier, inc=1, device_id=(other_band(step), var), device_id_type=MESH
        )

    loads = [
        pltpu.make_async_copy(source, target, load.at[index])
        for index, (source, target) in enumerate(
            ((wk_any, wk), (wq_any, wq), (wv_any, wv), (wo_any, wo), (up_any, up))
        )
    ]
    for item in loads:
        item.start()
    pl.semaphore_wait(barrier, bands + parts - 2 + corners)
    for step in range(1, parts):
        send_mix(step).start()
    rim_start()
    rim_ref[1, 1 : field_ref.shape[0] + 1] = field_ref[...]
    mixed = mix_ref[...].astype(jnp.float32)
    for step in range(1, parts):
        send_mix(step).wait_recv()
        mixed = mixed + mixes[step].astype(jnp.float32)
    scale = lax.rsqrt(jnp.mean(mixed * mixed, axis=-1, keepdims=True) + 1e-05)
    normed[...] = (mixed * scale * gain_ref[...]).astype(jnp.bfloat16)

    def project(weight):
        return jnp.dot(
            normed[...], weight[...], preferred_element_type=jnp.float32
        ).astype(jnp.bfloat16)

    loads[0].wait()
    key[...] = project(wk)

    @pl.loop(1, bands)
    def _(step):
        send_rows(key, key_all, key_out, key_in, step).start()

    loads[1].wait()
    query[...] = project(wq)

    @pl.loop(1, heads)
    def _(step):
        send_query(step).start()

    loads[2].wait()
    value[...] = project(wv)

    @pl.loop(1, bands)
    def _(step):
        send_rows(value, value_all, value_out, value_in, step).start()

    key_all[lines(band, rows), :] = key[:, columns(head)]
    value_all[lines(band, rows), :] = value[:, columns(head)]
    query_all[lines(head, rows), :] = query[:, columns(head)]

    def arrived(source, target, out_sem, in_sem, step):
        peer = lax.rem(band - step + bands, bands)
        return remote(
            source.at[:, columns(head)],
            target.at[lines(peer, rows)],
            out_sem.at[step], in_sem.at[step], other_band(step), var,
        )

    def arrived_query(step):
        peer = lax.rem(head - step + heads, heads)
        return remote(
            query.at[:, columns(head)],
            query_all.at[lines(peer, rows)],
            query_out.at[step], query_in.at[step], first + other_head(step), var,
        )

    @pl.loop(1, bands)
    def _(step):
        arrived(key, key_all, key_out, key_in, step).wait_recv()

    @pl.loop(1, heads)
    def _(step):
        arrived_query(step).wait_recv()

    group = max(1, min(heads, 256 // rows))
    size = group * rows
    for index in range(heads // group):
        scores = lax.dot_general(
            query_all[index * size : (index + 1) * size, :],
            key_all[...],
            (((1,), (1,)), ((), ())),
            preferred_element_type=jnp.float32,
        ) * (1.0 / math.sqrt(HD))
        weights = jnp.exp(scores - jnp.max(scores, axis=1, keepdims=True))
        total = jnp.sum(weights, axis=1, keepdims=True)
        probs = weights.astype(jnp.bfloat16)
        if index == 0:

            @pl.loop(1, bands)
            def _(step):
                arrived(value, value_all, value_out, value_in, step).wait_recv()

        update = jnp.dot(probs, value_all[...], preferred_element_type=jnp.float32)
        context[index * size : (index + 1) * size, :] = (update / total).astype(jnp.bfloat16)

        @pl.loop(index * group, (index + 1) * group)
        def _(peer):
            @pl.when(peer != head)
            def _():
                send_context(peer).start()

    joined[:, columns(head)] = context[lines(head, rows), :]
    loads[3].wait()
    loads[4].wait()

    @pl.loop(1, heads)
    def _(step):
        take_context(other_head(step)).wait_recv()

    partial[...] = jnp.dot(
        joined[...], wo[...], preferred_element_type=jnp.float32
    ).astype(jnp.bfloat16)
    for step in range(1, parts):
        send_slab(step).start()
    hidden = partial[lines(var, slab_rows), :].astype(jnp.float32)
    for step in range(1, parts):
        send_slab(step).wait_recv()
        hidden = hidden + slabs[step].astype(jnp.float32)
    hidden = (hidden + normed[lines(var, slab_rows), :].astype(jnp.float32)).astype(jnp.bfloat16)
    o_ref[16 : 16 + slab_rows, middle : 3 * middle] = jnp.dot(
        hidden, up[...], preferred_element_type=jnp.float32
    ).astype(jnp.bfloat16)
    fine_start()
    rim_take()
    rim_finish()

    for step in range(1, parts):
        send_mix(step).wait_send()
        send_slab(step).wait_send()

    @pl.loop(1, bands)
    def _(step):
        send_rows(key, key_all, key_out, key_in, step).wait_send()
        send_rows(value, value_all, value_out, value_in, step).wait_send()

    @pl.loop(1, heads)
    def _(step):
        send_query(step).wait_send()
        send_context(other_head(step)).wait_send()

    fine_take()
    fine_finish()


def token_stage(own_mix, agg_gain, field, wq, wk, wv, wo, w_up, bands, parts):
    rows = own_mix.shape[0]
    wide = wq.shape[1]
    heads = wide // HD
    fine = w_up.shape[1]

    def half(*shape):
        return pltpu.VMEM(shape, jnp.bfloat16)

    def flags(count):
        return pltpu.SemaphoreType.DMA((count,))

    vmem = pl.BlockSpec(memory_space=pltpu.VMEM)
    return pl.pallas_call(
        functools.partial(token_kernel, bands, heads, parts),
        out_shape=(
            jax.ShapeDtypeStruct((rows // parts + 32, 2 * fine), jnp.bfloat16),
            rim_shape(field),
        ),
        in_specs=[vmem] * 3 + [pl.BlockSpec(memory_space=pl.ANY)] * 5,
        out_specs=(vmem, vmem),
        scratch_shapes=[
            half(D, wide), half(D, wide), half(D, wide), half(wide, D), half(D, fine),
            half(parts, rows, D), half(rows, D),
            half(rows, wide), half(rows, wide), half(rows, wide),
            half(heads * rows, HD), half(bands * rows, HD), half(bands * rows, HD),
            half(heads * rows, HD), half(rows, wide), half(rows, D),
            half(parts, rows // parts, D),
            flags(5), flags(parts), flags(parts), flags(bands), flags(bands), flags(bands),
            flags(bands), flags(heads), flags(heads), flags(heads), flags(heads),
            flags(parts), flags(parts), flags(8), flags(8), flags(8), flags(8),
        ],
        compiler_params=pltpu.CompilerParams(
            collective_id=1, has_side_effects=True, vmem_limit_bytes=56 << 20
        ),
    )(own_mix, agg_gain[None], field, wq, wk, wv, wo, w_up)


def on_device(
    patches, w_embed, var_bias, agg_gain, wq, wk, wv, wo, w_up, conv1, bias1, conv2, cotangent
):
    var_count = lax.axis_size("var")
    band_count = lax.axis_size("band")
    var_local, lat_dev, lon_all, patch_len = patches.shape
    lon_dev = lon_all // var_count
    flattened = jnp.transpose(patches, (1, 2, 0, 3)).reshape(
        lat_dev * lon_all, var_local * patch_len
    )
    partial_mix = jnp.dot(
        flattened, w_embed.reshape(var_local * patch_len, D), preferred_element_type=jnp.float32
    )
    own_mix = (partial_mix + jnp.sum(var_bias, axis=0)).astype(jnp.bfloat16)
    token_rows = jnp.transpose(
        own_mix.reshape(lat_dev, var_count, lon_dev, D), (1, 0, 2, 3)
    ).reshape(-1, D)
    around, rim = token_stage(
        token_rows, agg_gain, cotangent, wq, wk, wv, wo, w_up, band_count, var_count
    )
    height = lat_dev * R
    width = lon_dev * R
    fine_wide = jnp.transpose(
        around.reshape(lon_dev + 32, 2 * R, R, C), (1, 3, 0, 2)
    ).reshape(2 * R, C, width + 32 * R)
    widened = fine_wide[:, :, 16 * R - 2 : 16 * R + width + 2]
    upsampled = fine_wide[2 : 2 + height, :, 16 * R : 16 * R + width]
    bias_cols = bias1[None, :, None]
    pre_wide = conv_padded(widened, conv1, height + 2, width + 2) + bias_cols
    row_ids = lax.axis_index("band") * height + jnp.arange(height + 2) - 1
    col_ids = lax.axis_index("var") * width + jnp.arange(width + 2) - 1
    rows_inside = (row_ids >= 0) & (row_ids < height * band_count)
    cols_inside = (col_ids >= 0) & (col_ids < width * var_count)
    inside = rows_inside[:, None, None] & cols_inside[None, None, :]
    active_pad = jnp.where(inside, jax.nn.gelu(pre_wide), 0.0).astype(jnp.bfloat16)
    fine_pad = widened[1:-1, :, 1:-1]
    pre = pre_wide[1:-1, :, 1:-1]
    field_out = (
        conv_padded(active_pad, conv2, height, width) + upsampled.astype(jnp.float32)
    ).astype(jnp.bfloat16)
    cotangent_pad = padded_from(rim)
    d_active = conv_padded(cotangent_pad, flipped(conv2), height, width)
    d_pre = jax.vjp(jax.nn.gelu, pre)[1](d_active)[0].astype(jnp.bfloat16)
    factor = 1.0 / math.sqrt(height * band_count * width * var_count)
    first_terms = weight_grad(fine_pad, d_pre).reshape(9 * C, C) * factor
    second_terms = weight_grad(active_pad, cotangent).reshape(9 * C, C) * factor
    bias_terms = jnp.sum(d_pre.astype(jnp.float32), axis=(0, 2)) * factor
    terms = jnp.concatenate([first_terms, second_terms], axis=1)
    bias_row = jnp.pad(bias_terms, (0, C))[None]
    summed, d_pre_pad = sum_everywhere(
        jnp.concatenate([terms, bias_row], axis=0), d_pre, band_count, var_count
    )
    grad_fine = (
        cotangent.astype(jnp.float32) + conv_padded(d_pre_pad, flipped(conv1), height, width)
    ).astype(jnp.bfloat16)
    grad_conv1 = summed[: 9 * C, :C].reshape(9, C, C)
    grad_conv2 = summed[: 9 * C, C:].reshape(9, C, C)
    grad_bias = summed[9 * C, :C]
    return (field_out, grad_fine, grad_conv1, grad_conv2, grad_bias)


def solution(mesh):
    in_specs = (
        P("var", "band", None, None),
        P("var", None, None),
        P("var", None),
        P(),
        P(None, "var"),
        P(None, "var"),
        P(None, "var"),
        P("var", None),
        P(),
        P(),
        P(),
        P(),
        P("band", None, "var"),
    )
    out_specs = (P("band", None, "var"), P("band", None, "var"), P(), P(), P())
    return jax.shard_map(
        on_device, mesh=mesh, in_specs=in_specs, out_specs=out_specs, check_vma=False
    )
```

```python
import functools
import math

import jax
import jax.numpy as jnp
from jax import lax
from jax.experimental import pallas as pl
from jax.experimental.pallas import tpu as pltpu
from jax.sharding import PartitionSpec as P

MESH = pl.DeviceIdType.MESH

D = 2048
HD = 128
C = 64
R = 4


def tap_stack(padded, height, width):
    pieces = [
        padded[row_tap : row_tap + height, :, col_tap : col_tap + width]
        for row_tap in range(3)
        for col_tap in range(3)
    ]
    return jnp.concatenate(pieces, axis=1)


def conv_padded(padded, weight, height, width):
    stacked = tap_stack(padded, height, width)
    return jnp.einsum(
        "ykx,ko->yox",
        stacked,
        weight.reshape(-1, weight.shape[2]),
        preferred_element_type=jnp.float32,
    )


def conv_by_rows(padded, weight, height, width):
    columns = jnp.concatenate([padded[:, :, tap : tap + width] for tap in range(3)], axis=1)
    rows = weight.reshape(3, -1, weight.shape[2])
    total = None
    for tap in range(3):
        term = jnp.einsum(
            "ykx,ko->yox",
            columns[tap : tap + height],
            rows[tap],
            preferred_element_type=jnp.float32,
        )
        total = term if total is None else total + term
    return total


def flipped(weight):
    return jnp.transpose(weight[::-1], (0, 2, 1))


def weight_grad(padded, grads):
    stacked = tap_stack(padded, grads.shape[0], grads.shape[2])
    summed = jnp.einsum("ykx,yox->ko", stacked, grads, preferred_element_type=jnp.float32)
    return summed.reshape(9, padded.shape[1], grads.shape[1])


SIDES = [(down, right) for down in (-1, 0, 1) for right in (-1, 0, 1) if down or right]


def present(bands, parts, down, right):
    band = lax.axis_index("band") + down
    var = lax.axis_index("var") + right
    return (band >= 0) & (band < bands) & (var >= 0) & (var < parts)


def to_sides(bands, parts, pieces, out_sem, in_sem):
    copies = []
    for index, (down, right) in enumerate(SIDES):
        source, target = pieces(down, right)
        copies.append(
            pltpu.make_async_remote_copy(
                src_ref=source,
                dst_ref=target,
                send_sem=out_sem.at[index],
                recv_sem=in_sem.at[index],
                device_id=(lax.axis_index("band") + down, lax.axis_index("var") + right),
                device_id_type=MESH,
            )
        )

    def start():
        for copy, (down, right) in zip(copies, SIDES):
            pl.when(present(bands, parts, down, right))(copy.start)

    def take():
        for copy, (down, right) in zip(copies, SIDES):
            pl.when(present(bands, parts, -down, -right))(copy.wait_recv)

    def finish():
        for copy, (down, right) in zip(copies, SIDES):
            pl.when(present(bands, parts, down, right))(copy.wait_send)

    return start, take, finish


def rim_pieces(field, rim):
    height = field.shape[0]

    def pieces(down, right):
        take, put = {-1: (0, height + 1), 0: (0, 1), 1: (height - 1, 0)}[down]
        size = 1 if down else height
        return field.at[pl.ds(take, size)], rim.at[1 - right, pl.ds(put, size)]

    return pieces


def rim_shape(field):
    return jax.ShapeDtypeStruct((3, field.shape[0] + 2) + field.shape[1:], field.dtype)


def padded_from(rim):
    return jnp.concatenate([rim[0, :, :, -1:], rim[1], rim[2, :, :, :1]], axis=2)


def sum_kernel(
    count, var_count, x_ref, field_ref, o_ref, rim_ref,
    paired, sums, landed, pair_out, pair_in, send1, recv1, send2, recv2, rim_out, rim_in,
):
    rim_ref[...] = jnp.zeros_like(rim_ref)
    rim_start, rim_take, rim_finish = to_sides(
        count // var_count, var_count, rim_pieces(field_ref, rim_ref), rim_out, rim_in
    )
    me = lax.axis_index("band") * var_count + lax.axis_index("var")

    def place(device):
        return (lax.div(device, var_count), lax.rem(device, var_count))

    half = count // 2
    band = lax.axis_index("band")
    core = lax.rem(band, 2)
    group = lax.div(band, 2) * var_count + lax.axis_index("var")
    mine = core * half

    def in_group(index):
        return (lax.div(index, var_count) * 2 + core, lax.rem(index, var_count))

    def remote(source, target, out_sem, in_sem, device):
        return pltpu.make_async_remote_copy(
            src_ref=source,
            dst_ref=target,
            send_sem=out_sem,
            recv_sem=in_sem,
            device_id=device,
            device_id_type=MESH,
        )

    partner = (band + 1 - 2 * core, lax.axis_index("var"))

    def give_half():
        theirs = pl.ds((1 - core) * half, half)
        return remote(x_ref.at[theirs], paired, pair_out.at[0], pair_in.at[0], partner)

    def share_half(owner):
        part = pl.ds(owner * half, half)
        return remote(o_ref.at[part], o_ref.at[part], pair_out.at[1], pair_in.at[1], partner)

    def scatter(step):
        peer = lax.rem(group + step, half)
        return remote(
            sums.at[peer], landed.at[step], send1.at[step], recv1.at[step], in_group(peer)
        )

    def spread(step, owner):
        peer = lax.rem(group + step, half)
        slot = o_ref.at[mine + owner]
        return remote(slot, slot, send2.at[step], recv2.at[step], in_group(peer))

    barrier = pltpu.get_barrier_semaphore()

    @pl.loop(1, count)
    def _(step):
        pl.semaphore_signal(
            barrier, inc=1, device_id=place(lax.rem(me + step, count)), device_id_type=MESH
        )

    pl.semaphore_wait(barrier, count - 1)
    give_half().start()
    rim_start()
    rim_ref[1, 1 : field_ref.shape[0] + 1] = field_ref[...]

    give_half().wait_recv()

    @pl.loop(0, half)
    def _(index):
        sums[index] = x_ref[mine + index] + paired[index]

    @pl.loop(1, half)
    def _(step):
        scatter(step).start()

    def add(step, total):
        scatter(step).wait_recv()
        return total + landed[step]

    o_ref[mine + group] = lax.fori_loop(1, half, add, sums[group])

    @pl.loop(1, half)
    def _(step):
        spread(step, group).start()

    @pl.loop(1, half)
    def _(step):
        spread(step, lax.rem(group - step + half, half)).wait_recv()

    share_half(core).start()
    give_half().wait_send()

    @pl.loop(1, half)
    def _(step):
        scatter(step).wait_send()
        spread(step, group).wait_send()

    share_half(1 - core).wait_recv()
    share_half(core).wait_send()
    rim_take()
    rim_finish()


def sum_everywhere(terms, field, band_count, var_count):
    count = band_count * var_count
    rows = -(-terms.shape[0] // (8 * count)) * 8
    padded = jnp.pad(terms, ((0, rows * count - terms.shape[0]), (0, 0)))
    slots = (count, rows, terms.shape[1])
    vmem = pl.BlockSpec(memory_space=pltpu.VMEM)
    summed, rim = pl.pallas_call(
        functools.partial(sum_kernel, count, var_count),
        out_shape=(jax.ShapeDtypeStruct(slots, jnp.float32), rim_shape(field)),
        in_specs=[vmem, vmem],
        out_specs=(vmem, vmem),
        scratch_shapes=[pltpu.VMEM((count // 2,) + slots[1:], jnp.float32) for _ in range(3)]
        + [pltpu.SemaphoreType.DMA((2,)) for _ in range(2)]
        + [pltpu.SemaphoreType.DMA((count // 2,)) for _ in range(4)]
        + [pltpu.SemaphoreType.DMA((8,)) for _ in range(2)],
        compiler_params=pltpu.CompilerParams(
            collective_id=0, has_side_effects=True, vmem_limit_bytes=32 << 20
        ),
    )(padded.reshape(slots), field)
    return summed.reshape(rows * count, terms.shape[1]), padded_from(rim)


def token_kernel(
    bands, heads, parts,
    mix_ref, gain_ref, field_ref, wq_any, wk_any, wv_any, wo_any, up_any,
    o_ref, rim_ref,
    wq, wk, wv, wo, up, mixes, normed, query, key, value, query_all, key_all, value_all,
    context, joined, partial, slabs,
    load, mix_out, mix_in, key_out, key_in, value_out, value_in, query_out, query_in,
    context_out, context_in, slab_out, slab_in, rim_out, rim_in, fine_out, fine_in,
):
    o_ref[...] = jnp.zeros_like(o_ref)
    rim_ref[...] = jnp.zeros_like(rim_ref)
    rim_start, rim_take, rim_finish = to_sides(
        bands, parts, rim_pieces(field_ref, rim_ref), rim_out, rim_in
    )
    band = lax.axis_index("band")
    var = lax.axis_index("var")
    rows = mix_ref.shape[0]
    slab_rows = rows // parts
    head = lax.rem(band, heads)
    first = band - head

    def columns(index):
        return pl.ds(pl.multiple_of(index * HD, HD), HD)

    def lines(index, size):
        return pl.ds(pl.multiple_of(index * size, size), size)

    def remote(src, dst, out_sem, in_sem, to_band, to_var):
        return pltpu.make_async_remote_copy(
            src_ref=src, dst_ref=dst, send_sem=out_sem, recv_sem=in_sem,
            device_id=(to_band, to_var), device_id_type=MESH,
        )

    def other_band(step):
        return lax.rem(band + step, bands)

    def other_head(step):
        return lax.rem(head + step, heads)

    def other_var(step):
        return lax.rem(var + step, parts)

    def send_mix(step):
        return remote(
            mix_ref, mixes.at[step], mix_out.at[step], mix_in.at[step], band, other_var(step)
        )

    def send_rows(source, target, out_sem, in_sem, step):
        peer = other_band(step)
        return remote(
            source.at[:, columns(lax.rem(peer, heads))],
            target.at[lines(band, rows)],
            out_sem.at[step], in_sem.at[step], peer, var,
        )

    def send_query(step):
        peer = other_head(step)
        return remote(
            query.at[:, columns(peer)],
            query_all.at[lines(head, rows)],
            query_out.at[step], query_in.at[step], first + peer, var,
        )

    def send_context(peer):
        return remote(
            context.at[lines(peer, rows)],
            joined.at[:, columns(head)],
            context_out.at[peer], context_in.at[head], first + peer, var,
        )

    def take_context(owner):
        return remote(
            context.at[lines(owner, rows)],
            joined.at[:, columns(owner)],
            context_out.at[owner], context_in.at[owner], first + owner, var,
        )

    def send_slab(step):
        peer = other_var(step)
        return remote(
            partial.at[lines(peer, slab_rows)],
            slabs.at[step],
            slab_out.at[step], slab_in.at[step], band, peer,
        )

    middle = up_any.shape[1] // 2

    def fine_pieces(down, right):
        take, put = {-1: (1, 3), 0: (1, 1), 1: (2, 0)}[down]
        size = middle if down else 2 * middle
        start, land, length = {
            -1: (16, 16 + slab_rows, 16),
            0: (16, 16, slab_rows),
            1: (slab_rows, 0, 16),
        }[right]
        return (
            o_ref.at[pl.ds(start, length), pl.ds(take * middle, size)],
            o_ref.at[pl.ds(land, length), pl.ds(put * middle, size)],
        )

    fine_start, fine_take, fine_finish = to_sides(bands, parts, fine_pieces, fine_out, fine_in)
    barrier = pltpu.get_barrier_semaphore()
    corners = 0
    for down, right in SIDES:
        if down and right:
            there = present(bands, parts, down, right)
            corners = corners + there.astype(jnp.int32)

            @pl.when(there)
            def _():
                pl.semaphore_signal(
                    barrier, inc=1, device_id=(band + down, var + right), device_id_type=MESH
                )

    @pl.loop(1, parts)
    def _(step):
        pl.semaphore_signal(
            barrier, inc=1, device_id=(band, other_var(step)), device_id_type=MESH
        )

    @pl.loop(1, bands)
    def _(step):
        pl.semaphore_signal(
            barrier, inc=1, device_id=(other_band(step), var), device_id_type=MESH
        )

    loads = [
        pltpu.make_async_copy(source, target, load.at[index])
        for index, (source, target) in enumerate(
            ((wk_any, wk), (wq_any, wq), (wv_any, wv), (wo_any, wo), (up_any, up))
        )
    ]
    for item in loads:
        item.start()
    pl.semaphore_wait(barrier, bands + parts - 2 + corners)
    for step in range(1, parts):
        send_mix(step).start()
    rim_start()
    rim_ref[1, 1 : field_ref.shape[0] + 1] = field_ref[...]
    mixed = mix_ref[...].astype(jnp.float32)
    for step in range(1, parts):
        send_mix(step).wait_recv()
        mixed = mixed + mixes[step].astype(jnp.float32)
    scale = lax.rsqrt(jnp.mean(mixed * mixed, axis=-1, keepdims=True) + 1e-05)
    normed[...] = (mixed * scale * gain_ref[...]).astype(jnp.bfloat16)

    def project(weight):
        return jnp.dot(
            normed[...], weight[...], preferred_element_type=jnp.float32
        ).astype(jnp.bfloat16)

    loads[0].wait()
    key[...] = project(wk)

    @pl.loop(1, bands)
    def _(step):
        send_rows(key, key_all, key_out, key_in, step).start()

    loads[1].wait()
    query[...] = project(wq)

    @pl.loop(1, heads)
    def _(step):
        send_query(step).start()

    loads[2].wait()
    value[...] = project(wv)

    @pl.loop(1, bands)
    def _(step):
        send_rows(value, value_all, value_out, value_in, step).start()

    key_all[lines(band, rows), :] = key[:, columns(head)]
    value_all[lines(band, rows), :] = value[:, columns(head)]
    query_all[lines(head, rows), :] = query[:, columns(head)]

    def arrived(source, target, out_sem, in_sem, step):
        peer = lax.rem(band - step + bands, bands)
        return remote(
            source.at[:, columns(head)],
            target.at[lines(peer, rows)],
            out_sem.at[step], in_sem.at[step], other_band(step), var,
        )

    def arrived_query(step):
        peer = lax.rem(head - step + heads, heads)
        return remote(
            query.at[:, columns(head)],
            query_all.at[lines(peer, rows)],
            query_out.at[step], query_in.at[step], first + other_head(step), var,
        )

    @pl.loop(1, bands)
    def _(step):
        arrived(key, key_all, key_out, key_in, step).wait_recv()

    @pl.loop(1, heads)
    def _(step):
        arrived_query(step).wait_recv()

    group = max(1, min(heads, 256 // rows))
    size = group * rows
    for index in range(heads // group):
        scores = lax.dot_general(
            query_all[index * size : (index + 1) * size, :],
            key_all[...],
            (((1,), (1,)), ((), ())),
            preferred_element_type=jnp.float32,
        ) * (1.0 / math.sqrt(HD))
        weights = jnp.exp(scores - jnp.max(scores, axis=1, keepdims=True))
        total = jnp.sum(weights, axis=1, keepdims=True)
        probs = weights.astype(jnp.bfloat16)
        if index == 0:

            @pl.loop(1, bands)
            def _(step):
                arrived(value, value_all, value_out, value_in, step).wait_recv()

        update = jnp.dot(probs, value_all[...], preferred_element_type=jnp.float32)
        context[index * size : (index + 1) * size, :] = (update / total).astype(jnp.bfloat16)

        @pl.loop(index * group, (index + 1) * group)
        def _(peer):
            @pl.when(peer != head)
            def _():
                send_context(peer).start()

    joined[:, columns(head)] = context[lines(head, rows), :]
    loads[3].wait()
    loads[4].wait()

    @pl.loop(1, heads)
    def _(step):
        take_context(other_head(step)).wait_recv()

    partial[...] = jnp.dot(
        joined[...], wo[...], preferred_element_type=jnp.float32
    ).astype(jnp.bfloat16)
    for step in range(1, parts):
        send_slab(step).start()
    hidden = partial[lines(var, slab_rows), :].astype(jnp.float32)
    for step in range(1, parts):
        send_slab(step).wait_recv()
        hidden = hidden + slabs[step].astype(jnp.float32)
    hidden = (hidden + normed[lines(var, slab_rows), :].astype(jnp.float32)).astype(jnp.bfloat16)
    o_ref[16 : 16 + slab_rows, middle : 3 * middle] = jnp.dot(
        hidden, up[...], preferred_element_type=jnp.float32
    ).astype(jnp.bfloat16)
    fine_start()
    rim_take()
    rim_finish()

    for step in range(1, parts):
        send_mix(step).wait_send()
        send_slab(step).wait_send()

    @pl.loop(1, bands)
    def _(step):
        send_rows(key, key_all, key_out, key_in, step).wait_send()
        send_rows(value, value_all, value_out, value_in, step).wait_send()

    @pl.loop(1, heads)
    def _(step):
        send_query(step).wait_send()
        send_context(other_head(step)).wait_send()

    fine_take()
    fine_finish()


def token_stage(own_mix, agg_gain, field, wq, wk, wv, wo, w_up, bands, parts):
    rows = own_mix.shape[0]
    wide = wq.shape[1]
    heads = wide // HD
    fine = w_up.shape[1]

    def half(*shape):
        return pltpu.VMEM(shape, jnp.bfloat16)

    def flags(count):
        return pltpu.SemaphoreType.DMA((count,))

    vmem = pl.BlockSpec(memory_space=pltpu.VMEM)
    return pl.pallas_call(
        functools.partial(token_kernel, bands, heads, parts),
        out_shape=(
            jax.ShapeDtypeStruct((rows // parts + 32, 2 * fine), jnp.bfloat16),
            rim_shape(field),
        ),
        in_specs=[vmem] * 3 + [pl.BlockSpec(memory_space=pl.ANY)] * 5,
        out_specs=(vmem, vmem),
        scratch_shapes=[
            half(D, wide), half(D, wide), half(D, wide), half(wide, D), half(D, fine),
            half(parts, rows, D), half(rows, D),
            half(rows, wide), half(rows, wide), half(rows, wide),
            half(heads * rows, HD), half(bands * rows, HD), half(bands * rows, HD),
            half(heads * rows, HD), half(rows, wide), half(rows, D),
            half(parts, rows // parts, D),
            flags(5), flags(parts), flags(parts), flags(bands), flags(bands), flags(bands),
            flags(bands), flags(heads), flags(heads), flags(heads), flags(heads),
            flags(parts), flags(parts), flags(8), flags(8), flags(8), flags(8),
        ],
        compiler_params=pltpu.CompilerParams(
            collective_id=1, has_side_effects=True, vmem_limit_bytes=56 << 20
        ),
    )(own_mix, agg_gain[None], field, wq, wk, wv, wo, w_up)


def on_device(
    patches, w_embed, var_bias, agg_gain, wq, wk, wv, wo, w_up, conv1, bias1, conv2, cotangent
):
    var_count = lax.axis_size("var")
    band_count = lax.axis_size("band")
    var_local, lat_dev, lon_all, patch_len = patches.shape
    lon_dev = lon_all // var_count
    flattened = jnp.transpose(patches, (1, 2, 0, 3)).reshape(
        lat_dev * lon_all, var_local * patch_len
    )
    partial_mix = jnp.dot(
        flattened, w_embed.reshape(var_local * patch_len, D), preferred_element_type=jnp.float32
    )
    own_mix = (partial_mix + jnp.sum(var_bias, axis=0)).astype(jnp.bfloat16)
    token_rows = jnp.transpose(
        own_mix.reshape(lat_dev, var_count, lon_dev, D), (1, 0, 2, 3)
    ).reshape(-1, D)
    around, rim = token_stage(
        token_rows, agg_gain, cotangent, wq, wk, wv, wo, w_up, band_count, var_count
    )
    height = lat_dev * R
    width = lon_dev * R
    fine_wide = jnp.transpose(
        around.reshape(lon_dev + 32, 2 * R, R, C), (1, 3, 0, 2)
    ).reshape(2 * R, C, width + 32 * R)
    widened = fine_wide[:, :, 16 * R - 2 : 16 * R + width + 2]
    upsampled = fine_wide[2 : 2 + height, :, 16 * R : 16 * R + width]
    bias_cols = bias1[None, :, None]
    pre_wide = conv_by_rows(widened, conv1, height + 2, width + 2) + bias_cols
    row_ids = lax.axis_index("band") * height + jnp.arange(height + 2) - 1
    col_ids = lax.axis_index("var") * width + jnp.arange(width + 2) - 1
    rows_inside = (row_ids >= 0) & (row_ids < height * band_count)
    cols_inside = (col_ids >= 0) & (col_ids < width * var_count)
    inside = rows_inside[:, None, None] & cols_inside[None, None, :]
    active_pad = jnp.where(inside, jax.nn.gelu(pre_wide), 0.0).astype(jnp.bfloat16)
    fine_pad = widened[1:-1, :, 1:-1]
    pre = pre_wide[1:-1, :, 1:-1]
    field_out = (
        conv_padded(active_pad, conv2, height, width) + upsampled.astype(jnp.float32)
    ).astype(jnp.bfloat16)
    cotangent_pad = padded_from(rim)
    d_active = conv_by_rows(cotangent_pad, flipped(conv2), height, width)
    d_pre = jax.vjp(jax.nn.gelu, pre)[1](d_active)[0].astype(jnp.bfloat16)
    factor = 1.0 / math.sqrt(height * band_count * width * var_count)
    first_terms = weight_grad(fine_pad, d_pre).reshape(9 * C, C) * factor
    second_terms = weight_grad(active_pad, cotangent).reshape(9 * C, C) * factor
    bias_terms = jnp.sum(d_pre.astype(jnp.float32), axis=(0, 2)) * factor
    terms = jnp.concatenate([first_terms, second_terms], axis=1)
    bias_row = jnp.pad(bias_terms, (0, C))[None]
    summed, d_pre_pad = sum_everywhere(
        jnp.concatenate([terms, bias_row], axis=0), d_pre, band_count, var_count
    )
    grad_fine = (
        cotangent.astype(jnp.float32) + conv_by_rows(d_pre_pad, flipped(conv1), height, width)
    ).astype(jnp.bfloat16)
    grad_conv1 = summed[: 9 * C, :C].reshape(9, C, C)
    grad_conv2 = summed[: 9 * C, C:].reshape(9, C, C)
    grad_bias = summed[9 * C, :C]
    return (field_out, grad_fine, grad_conv1, grad_conv2, grad_bias)


def solution(mesh):
    in_specs = (
        P("var", "band", None, None),
        P("var", None, None),
        P("var", None),
        P(),
        P(None, "var"),
        P(None, "var"),
        P(None, "var"),
        P("var", None),
        P(),
        P(),
        P(),
        P(),
        P("band", None, "var"),
    )
    out_specs = (P("band", None, "var"), P("band", None, "var"), P(), P(), P())
    return jax.shard_map(
        on_device, mesh=mesh, in_specs=in_specs, out_specs=out_specs, check_vma=False
    )
```
